32 devices in a mesh: groups: 2 (over y), axial: 8 (over z, x), dp: 2 (over core).
Axes of the slice: x: 2, y: 2, z: 4, core: 2. Of those that a mesh axis runs over, the one named last changes fastest.
Arguments:
- pair: bfloat16 [4, 48, 48, 128], P(('groups', 'dp'), 'axial'), parts along dimension 0, may hold values from -6 to 6
- pair_mask: int32 [4, 48, 48], P(('groups', 'dp'), 'axial'), parts along dimension 0, may hold values from 0 to 1, as said below
- ln_gain: float32 [2, 128], replicated, may hold values from 0.5 to 1.5
- projection_weight: bfloat16 [2, 128, 512], replicated, may hold values from -0.5 to 0.5
- pair_bias_weight: bfloat16 [2, 128, 4], replicated, may hold values from -128 to 128
- w_out: bfloat16 [2, 128, 128], replicated, may hold values from -0.5 to 0.5
- cotangent: bfloat16 [4, 48, 48, 128], P(('groups', 'dp'), None, 'axial'), parts along dimension 0, may hold values from -6 to 6
Outputs:
- pair_out: bfloat16 [4, 48, 48, 128], P(('groups', 'dp'), None, 'axial'), parts along dimension 0
- pair_grad: bfloat16 [4, 48, 48, 128], P(('groups', 'dp'), 'axial'), parts along dimension 0
- grad_ln_gain: float32 [4, 128], P('groups'), parts along dimension 0
- grad_w_proj: float32 [4, 128, 512], P('groups'), parts along dimension 0
- grad_w_bias: float32 [4, 128, 4], P('groups'), parts along dimension 0
- grad_w_out: float32 [4, 128, 128], P('groups'), parts along dimension 0
The draws below stay inside these ranges and needn't reach their ends.
There are 2 independent parts, one for each index of `groups`. The reference program is written for one: setup_inputs(seed, part) draws one part's arguments, and reference() takes and returns one part's arrays. A program takes and returns all parts, laid end to end along the dimension named above; an argument that names none is the same for every part. Nothing has to cross between parts.
Inputs may be any that keep to these rules, and one draw needn't show every extreme that they name: pair_mask[n, i, k] = t[n, i] * t[n, k], where t[n] is 1 on a leading run of the crop's positions and 0 after it; so the mask is symmetric.
All inputs are finite; a program needn't handle non-finite values.
Results may differ from the reference program's by a relative error of at most 0.0095.
The reference program's roundings to bfloat16 on the way count: a program that leaves them out, or rounds other values in their place, can miss the bound.
Values may be sent and summed in bfloat16 or wider, within the bound.
A program may use at most 128 MiB of HBM per device.

```python
import math
import jax
import jax.numpy as jnp
from jax import lax

C = 128
H = 4
DH = 32
HD = 128
ROW_DEV = 6
N = 48
CROPS = 2


def draw_pair_mask(key, part):
    key = jax.random.fold_in(key, 7)
    lengths = jax.random.randint(key, (CROPS,), N // 2, N + 1)
    tokens = (jnp.arange(N)[None, :] < lengths[:, None]).astype(jnp.int32)
    return tokens[:, :, None] * tokens[:, None, :]


def draw_pair_bias_weight(key, part):
    key = jax.random.fold_in(key, 11)
    base = jax.random.truncated_normal(key, -4.0, 4.0, (2, C, H), jnp.float32)
    factor = 1.5 * jnp.ones((H,), jnp.float32)
    return (base * factor / math.sqrt(C)).astype(jnp.bfloat16)


def level_of(stream_key, shape, shards, low, top_value):
    level, own = 1.0, jax.random.fold_in(stream_key, 6)
    for position, parts in shards:
        draws = jnp.exp(jax.random.uniform(jax.random.fold_in(own, position), (parts,), jnp.float32, low / len(shards), top_value / len(shards)))
        level = level * jnp.repeat(draws, shape[position] // parts).reshape([-1 if axis == position else 1 for axis in range(len(shape))])
    return level


def bell_draw(own_key, dims, deviation, limit, split=(), kind=jnp.bfloat16):
    values = deviation * jax.random.normal(own_key, dims, jnp.float32)
    if split:
        values = values * level_of(own_key, dims, split, -0.22, 0.18)
    return jnp.clip(values, -limit, limit).astype(kind)


def setup_inputs(seed: int = 0, part: int = 0) -> dict:
    splits = jax.random.split(jax.random.key(seed), 8)
    own_keys = jax.random.split(jax.random.fold_in(splits[7], part), 8)
    return {
        "pair": bell_draw(own_keys[0], (CROPS, N, N, C), 1.0, 6.0, ((0, 2), (1, 8))),
        "pair_mask": draw_pair_mask(jax.random.fold_in(jax.random.fold_in(splits[7], part), 71), part),
        "ln_gain": jnp.clip(1.0 + 0.1 * jax.random.normal(splits[2], (2, C), jnp.float32), 0.5, 1.5),
        "projection_weight": bell_draw(splits[3], (2, C, 4 * HD), C ** -0.5, 0.5),
        "pair_bias_weight": draw_pair_bias_weight(jax.random.fold_in(splits[7], 71), part),
        "w_out": bell_draw(splits[5], (2, HD, C), HD ** -0.5, 0.5),
        "cotangent": bell_draw(own_keys[6], (CROPS, N, N, C), 1.0, 6.0, ((0, 2), (2, 8))),
    }


eps = 1e-05
masked = -1000000000.0
highest = lax.Precision.HIGHEST

def mix(form, left, right):
    return jnp.einsum(form, left.astype(jnp.float32), right.astype(jnp.float32), precision=highest)

def apply_layer_norm(pair_input, norm_gain):
    values = pair_input.astype(jnp.float32)
    centered_input = values - lax.optimization_barrier(jnp.mean(values, axis=-1, keepdims=True))
    spread_values = lax.rsqrt(lax.optimization_barrier(jnp.mean(centered_input * centered_input, axis=-1, keepdims=True)) + eps)
    standardized_input = centered_input * spread_values
    return (standardized_input, spread_values, (standardized_input * norm_gain).astype(jnp.bfloat16))

def to_blocks(array):
    crops = array.shape[0]
    shaped = array.reshape((crops, N // ROW_DEV, ROW_DEV) + array.shape[2:])
    return jnp.moveaxis(shaped, 1, 0)

def from_blocks(array):
    joined = jnp.moveaxis(array, 0, 1)
    return joined.reshape((joined.shape[0], N) + joined.shape[3:])

def prepare_inputs(pair_input, norm_gain, projection_weight, pair_bias_weight):
    standardized_input, spread_values, normed_input = apply_layer_norm(pair_input, norm_gain)
    proj = mix('nijc,ce->nije', normed_input, projection_weight).astype(jnp.bfloat16)
    crops = pair_input.shape[0]
    block_list = to_blocks(proj.reshape(crops, N, N, 4, H, DH))
    bias_term = mix('njkc,ch->nhjk', normed_input, pair_bias_weight)
    return (standardized_input, spread_values, normed_input, block_list, bias_term)

def block_probs(query, keys, bias_term, keep_rows, scale):
    scores = mix('nabhd,nakhd->nahbk', query, keys) * scale + bias_term[:, None]
    scores = jnp.where(keep_rows[:, :, None, None, :], scores, masked)
    probs = jax.nn.softmax(scores, axis=-1)
    return (probs, probs.astype(jnp.bfloat16))

def attend_forward(pair_input, keep, norm_gain, projection_weight, pair_bias_weight, w_out):
    standardized_input, spread_values, normed_input, block_list, bias_term = prepare_inputs(pair_input, norm_gain, projection_weight, pair_bias_weight)
    scale = 1.0 / math.sqrt(DH)

    def one_block(carry, item):
        query, keys, values, keep_rows = item
        probs, probs_b = block_probs(query, keys, bias_term, keep_rows, scale)
        return (carry, mix('nahbk,nakhd->nabhd', probs_b, values))
    _, attended = lax.scan(one_block, jnp.float32(0.0), (block_list[:, :, :, :, 0], block_list[:, :, :, :, 1], block_list[:, :, :, :, 2], to_blocks(keep)))
    gate = jax.nn.sigmoid(block_list[:, :, :, :, 3].astype(jnp.float32))
    gated = from_blocks((gate * attended).astype(jnp.bfloat16))
    gated = gated.reshape(gated.shape[0], N, N, H * DH)
    delta = mix('nije,ec->nijc', gated, w_out)
    return (pair_input.astype(jnp.float32) + delta).astype(jnp.bfloat16)

def attend_backward(pair_input, grad_out, keep, norm_gain, projection_weight, pair_bias_weight, w_out):
    standardized_input, spread_values, normed_input, block_list, bias_term = prepare_inputs(pair_input, norm_gain, projection_weight, pair_bias_weight)
    scale = 1.0 / math.sqrt(DH)
    crops = pair_input.shape[0]
    d_gated = mix('nijc,ec->nije', grad_out, w_out).reshape(crops, N, N, H, DH)
    gate = jax.nn.sigmoid(block_list[:, :, :, :, 3].astype(jnp.float32))

    def one_block(d_bias, item):
        query, keys, values, keep_rows, gate_rows, d_rows = item
        probs, probs_b = block_probs(query, keys, bias_term, keep_rows, scale)
        attended = mix('nahbk,nakhd->nabhd', probs_b, values)
        gated = (gate_rows * attended).astype(jnp.bfloat16)
        d_att = (d_rows * gate_rows).astype(jnp.bfloat16)
        d_gate = (d_rows * attended * gate_rows * (1.0 - gate_rows)).astype(jnp.bfloat16)
        d_probs = mix('nabhd,nakhd->nahbk', d_att, values)
        total = lax.optimization_barrier(jnp.sum(probs * d_probs, axis=-1, keepdims=True))
        d_scores = jnp.where(keep_rows[:, :, None, None, :], probs * (d_probs - total), 0.0)
        d_scores_b = d_scores.astype(jnp.bfloat16)
        d_query = (mix('nahbk,nakhd->nabhd', d_scores_b, keys) * scale).astype(jnp.bfloat16)
        d_keys = (mix('nahbk,nabhd->nakhd', d_scores_b, query) * scale).astype(jnp.bfloat16)
        d_values = mix('nahbk,nabhd->nakhd', probs_b, d_att).astype(jnp.bfloat16)
        d_split = jnp.stack([d_query, d_keys, d_values, d_gate], axis=3)
        return (d_bias + lax.optimization_barrier(jnp.sum(d_scores, axis=1)), (d_split, gated))
    start = jnp.zeros((crops, H, N, N), jnp.float32)
    items = (block_list[:, :, :, :, 0], block_list[:, :, :, :, 1], block_list[:, :, :, :, 2], to_blocks(keep), gate, to_blocks(d_gated))
    d_bias, (d_split, gated) = lax.scan(one_block, start, items)
    d_proj = from_blocks(d_split).reshape(crops, N, N, 4 * H * DH)
    gated = from_blocks(gated).reshape(crops, N, N, H * DH)
    grad_w_out = mix('nije,nijc->ec', gated, grad_out)
    layer_norm_gradient = mix('nije,ce->nijc', d_proj, projection_weight) + mix('nhjk,ch->njkc', d_bias, pair_bias_weight)
    grad_w_proj = mix('nijc,nije->ce', normed_input, d_proj)
    grad_w_bias = mix('njkc,nhjk->ch', normed_input, d_bias)
    normalized_gradient = layer_norm_gradient * norm_gain
    gain_gradient = lax.optimization_barrier(jnp.sum(layer_norm_gradient * standardized_input, axis=(0, 1, 2)))
    inner_product = normalized_gradient - lax.optimization_barrier(jnp.mean(normalized_gradient, axis=-1, keepdims=True)) - standardized_input * lax.optimization_barrier(jnp.mean(normalized_gradient * standardized_input, axis=-1, keepdims=True))
    d_in = (grad_out.astype(jnp.float32) + spread_values * inner_product).astype(jnp.bfloat16)
    return (d_in, (gain_gradient, grad_w_proj, grad_w_bias, grad_w_out))

def reference(pair, pair_mask, ln_gain, projection_weight, pair_bias_weight, w_out, cotangent):
    keep = pair_mask > 0
    keep_t = jnp.swapaxes(keep, 1, 2)
    first = (ln_gain[0], projection_weight[0], pair_bias_weight[0], w_out[0])
    second = (ln_gain[1], projection_weight[1], pair_bias_weight[1], w_out[1])
    middle = attend_forward(pair, keep, *first)
    middle_t = jnp.swapaxes(middle, 1, 2)
    pair_out = jnp.swapaxes(attend_forward(middle_t, keep_t, *second), 1, 2)
    d_middle_t, grads_second = attend_backward(middle_t, jnp.swapaxes(cotangent, 1, 2), keep_t, *second)
    pair_grad, grads_first = attend_backward(pair, jnp.swapaxes(d_middle_t, 1, 2), keep, *first)
    stacked = [jnp.stack([grads_first[idx], grads_second[idx]]) for idx in range(4)]
    return (pair_out, pair_grad, stacked[0], stacked[1], stacked[2], stacked[3])
```

```python
import functools
import math

import jax
import jax.numpy as jnp
from jax import lax
from jax.experimental import pallas as pl
from jax.experimental.pallas import tpu as pltpu
from jax.sharding import PartitionSpec as P

MESH = pl.DeviceIdType.MESH
F32, BF16 = jnp.float32, jnp.bfloat16
H = 4
EPS = 1e-05
MASKED = -1000000000.0
HIGHEST = lax.Precision.HIGHEST


def dot(a, b, ca, cb, precision=None):
    return lax.dot_general(a, b, (((ca,), (cb,)), ((), ())), precision=precision, preferred_element_type=F32)


def kernel(
    n, rows, width, small, block, chunk,
    pair_ref, mask_ref, gain_ref, wproj_ref, wbias_ref, wout_ref, cot_ref, spread_ref, gather_ref,
    out_ref, grad_ref, gproj_ref, gout_ref, tail_ref,
    xhat, rstd, normed, proj, gate, att, dgated, gated, dproj, x2, dy1, bias, dacc, kept,
    bgat, dsend, drecv, asend, arecv, part, fromcore, half, red, full, tails,
    send_sem, recv_sem, core_send, core_recv,
):
    me = lax.axis_index("axial")
    core = lax.axis_index("dp")
    other = 1 - core
    channels = pair_ref.shape[1]
    head = channels // H
    scale = 1.0 / math.sqrt(head)
    stack = H if small else 1
    half_rows = n * chunk

    def slot_of(l):
        return l if small else 0

    def steps(low, high, body):
        if small:
            for idx in range(low, high):
                body(idx)
        else:
            lax.fori_loop(low, high, lambda idx, c: (body(idx), c)[1], 0)

    barrier = pltpu.get_barrier_semaphore()

    def greet(off):
        pl.semaphore_signal(barrier, inc=1, device_id={"axial": lax.rem(me + off, n)}, device_id_type=MESH)

    steps(1, n, greet)
    pl.semaphore_signal(barrier, inc=1, device_id={"dp": other}, device_id_type=MESH)

    def axial_copy(phase, off, source, target, slot):
        peer = lax.rem(me + off, n)
        return pltpu.make_async_remote_copy(
            src_ref=source(peer), dst_ref=target(slot),
            send_sem=send_sem.at[phase, off], recv_sem=recv_sem.at[phase, off],
            device_id={"axial": peer}, device_id_type=MESH,
        )

    def start(phase, source, target):
        steps(1, n, lambda off: axial_copy(phase, off, source, target, me).start())

    def finish(phase, source, target):
        steps(1, n, lambda off: axial_copy(phase, off, source, target, lax.rem(me + n - off, n)).wait())

    def core_copy(phase, source, target):
        return pltpu.make_async_remote_copy(
            src_ref=source, dst_ref=target, send_sem=core_send.at[phase], recv_sem=core_recv.at[phase],
            device_id={"dp": other}, device_id_type=MESH,
        )

    def at_row(a):
        return pl.ds(a * width if small else pl.multiple_of(a * width, 16), width)

    lanes = lax.broadcasted_iota(jnp.int32, (1, channels), 1)
    head_masks = [jnp.where((lanes >= h * head) & (lanes < (h + 1) * head), 1.0, 0.0) for h in range(H)]

    def stacked(value, first):
        value = value.astype(F32)
        return jnp.concatenate([value * head_masks[first + h] for h in range(stack)], axis=0).astype(BF16)

    def merged(value, first):
        total = value[:width] * head_masks[first]
        for h in range(1, stack):
            total = total + value[h * width : (h + 1) * width] * head_masks[first + h]
        return total

    def prepare(l, x_ref):
        x = x_ref[...].astype(F32)
        centered = x - jnp.mean(x, axis=-1, keepdims=True)
        spread = lax.rsqrt(jnp.mean(centered * centered, axis=-1, keepdims=True) + EPS)
        hat = centered * spread
        xhat[l] = hat
        rstd[l] = jnp.broadcast_to(spread, hat.shape)
        normed[l] = (hat * gain_ref[l : l + 1]).astype(BF16)

        def own_bias(a):
            bgat[slot_of(l), me * rows + a] = dot(wbias_ref[l], normed[l, at_row(a)], 1, 1)

        steps(0, rows, own_bias)

    def project(l):
        values = dot(normed[l], wproj_ref[l], 1, 0).astype(BF16)
        proj[l] = values
        gate[l] = jax.nn.sigmoid(values[:, 3 * channels :].astype(F32))

    def bias_source(l):
        return lambda peer: bgat.at[slot_of(l), pl.ds(me * rows, rows)]

    def bias_target(l):
        return lambda slot: bgat.at[slot_of(l), pl.ds(slot * rows, rows)]

    def stack_bias(l):
        for h in range(H):
            bias[l, h * width : (h + 1) * width] = bgat[slot_of(l), :, h, :]

    def probabilities(l, a, first, queries, keys):
        scores = dot(queries, keys, 1, 1) * scale + bias[l, first * width : (first + stack) * width]
        scores = jnp.where(mask_ref[pl.ds(a, 1)] > 0, scores, MASKED)
        top = jnp.max(scores, axis=-1, keepdims=True)
        weights = jnp.exp(scores - top)
        return weights * (1.0 / jnp.sum(weights, axis=-1, keepdims=True))

    def column(l, a, part_index):
        return proj[l, at_row(a), part_index * channels : (part_index + 1) * channels]

    def forward_row(a):
        keys, values, query = column(0, a, 1), column(0, a, 2), column(0, a, 0)
        total = None
        for first in range(0, H, stack):
            probs = probabilities(0, a, first, stacked(query, first), keys)
            if small:
                kept[a] = probs
            term = merged(dot(probs.astype(BF16), values, 1, 0), first)
            total = term if total is None else total + term
        att[0, at_row(a)] = total

    def backward_row(l, a):
        keys, values, query = column(l, a, 1), column(l, a, 2), column(l, a, 0)
        gates = gate[l, at_row(a)]
        d_row = dgated[at_row(a)]
        d_att = (d_row * gates).astype(BF16)
        keep = mask_ref[pl.ds(a, 1)] > 0
        total = d_query = d_keys = d_values = None
        for first in range(0, H, stack):
            queries = stacked(query, first)
            probs = kept[a] if small and l == 0 else probabilities(l, a, first, queries, keys)
            probs_b = probs.astype(BF16)
            d_stack = stacked(d_att, first)
            if l == 1:
                term = merged(dot(probs_b, values, 1, 0), first)
                total = term if total is None else total + term
            d_probs = dot(d_stack, values, 1, 1)
            inner = jnp.sum(probs * d_probs, axis=-1, keepdims=True)
            d_scores = jnp.where(keep, probs * (d_probs - inner), 0.0)
            where = slice(first * width, (first + stack) * width)
            if small and a == 0:
                dacc[where] = d_scores
            else:
                dacc[where] += d_scores
            d_b = d_scores.astype(BF16)
            terms = (merged(dot(d_b, keys, 1, 0), first), dot(d_b, queries, 0, 0), dot(probs_b, d_stack, 0, 0))
            if d_query is None:
                d_query, d_keys, d_values = terms
            else:
                d_query, d_keys, d_values = d_query + terms[0], d_keys + terms[1], d_values + terms[2]
        if l == 1:
            att[1, at_row(a)] = total
        else:
            total = att[0, at_row(a)]
        d_gate = d_row * total * gates * (1.0 - gates)
        dproj[at_row(a), :channels] = (d_query * scale).astype(BF16)
        dproj[at_row(a), channels : 2 * channels] = (d_keys * scale).astype(BF16)
        dproj[at_row(a), 2 * channels : 3 * channels] = d_values.astype(BF16)
        dproj[at_row(a), 3 * channels :] = d_gate.astype(BF16)

    def gate_output(l, x_ref):
        values = (gate[l] * att[l]).astype(BF16)
        gated[l] = values
        return (x_ref[...].astype(F32) + dot(values, wout_ref[l], 1, 0)).astype(BF16)

    def turn_send(index, value_at):
        def turned(base, length):
            total = None
            for a in range(rows):
                spots = lax.broadcasted_iota(jnp.int32, (length, width), 0) + (base - a)
                chosen = jnp.where(spots == spread_ref[...], 1.0, 0.0).astype(BF16)
                term = dot(chosen, value_at(a), 1, 0)
                total = term if total is None else total + term
            return total.astype(BF16)

        def one(peer):
            asend[slot_of(index), peer] = turned(peer * block, block)

        if small:
            asend[index] = turned(0, n * block).reshape(n, block, channels)
        else:
            steps(0, n, one)
        arecv[slot_of(index), me] = asend[slot_of(index), me]
        start(4 + index, lambda peer: asend.at[slot_of(index), peer], lambda slot: arecv.at[slot_of(index), slot])

    def turn_receive(index, target):
        finish(4 + index, lambda peer: asend.at[slot_of(index), peer], lambda slot: arecv.at[slot_of(index), slot])
        arrived = arecv[slot_of(index)].reshape(n * block, channels)

        def one(a):
            spots = lax.broadcasted_iota(jnp.int32, (width, n * block), 1) - a * rows
            chosen = jnp.where(spots == gather_ref[...], 1.0, 0.0).astype(BF16)
            target[at_row(a)] = dot(chosen, arrived, 1, 0).astype(BF16)

        steps(0, rows, one)

    def ds_source(l):
        return lambda peer: dsend.at[slot_of(l), pl.ds(peer * rows, rows)]

    def ds_target(l):
        return lambda slot: drecv.at[slot_of(l), slot]

    def send_bias_grad(l):
        for h in range(H):
            dsend[slot_of(l), :, h, :] = dacc[h * width : (h + 1) * width]
        drecv[slot_of(l), me] = dsend[slot_of(l), pl.ds(me * rows, rows)]
        start(2 + l, ds_source(l), ds_target(l))

    def weight_grads(l, dy):
        values = dot(normed[l], dproj[...], 0, 0)
        for e in range(4):
            part[l, e * channels : (e + 1) * channels] = values[:, e * channels : (e + 1) * channels]
        part[l, 4 * channels : 5 * channels] = dot(gated[l], dy, 0, 0)

    def core_first(l):
        return core_copy(l, part.at[l, pl.ds(other * half_rows, half_rows)], fromcore.at[l])

    def reduce_source(l):
        return lambda peer: half.at[l, peer]

    def reduce_target(l):
        return lambda slot: red.at[l, slot]

    def core_sum(l):
        core_first(l).wait()
        value = part[l, pl.ds(pl.multiple_of(core * half_rows, 8), half_rows)] + fromcore[l]
        half[l] = value.reshape(n, chunk, channels)
        red[l, me] = half[l, me]
        start(6 + l, reduce_source(l), reduce_target(l))

    def full_source(l):
        return lambda peer: full.at[l, core, me]

    def full_target(l):
        return lambda slot: full.at[l, core, slot]

    def axial_sum(l):
        finish(6 + l, reduce_source(l), reduce_target(l))
        full[l, core, me] = jnp.sum(red[l], axis=0)
        start(8 + l, full_source(l), full_target(l))

    def core_last(l):
        return core_copy(2 + l, full.at[l, core], full.at[l, core])

    def core_last_wait(l):
        return core_copy(2 + l, full.at[l, core], full.at[l, other])

    def layer_norm_grad(l, dn, dy):
        finish(2 + l, ds_source(l), ds_target(l))
        own = jnp.sum(drecv[slot_of(l)], axis=0)
        extra, bias_grad = [], None
        weights = wbias_ref[l].astype(F32)
        for a in range(rows):
            extra.append(dot(own[a], weights, 0, 0, HIGHEST))
            term = dot(own[a], normed[l, a * width : (a + 1) * width].astype(F32), 1, 0, HIGHEST)
            bias_grad = term if bias_grad is None else bias_grad + term
        dn = dn + jnp.concatenate(extra, axis=0)
        hat = xhat[l]
        gain_grad = jnp.sum(dn * hat, axis=0, keepdims=True)
        d_hat = dn * gain_ref[l : l + 1]
        inner = (
            d_hat
            - jnp.mean(d_hat, axis=-1, keepdims=True)
            - hat * jnp.mean(d_hat * hat, axis=-1, keepdims=True)
        )
        tails[me, l * 16 : l * 16 + 8] = bias_grad
        tails[me, l * 16 + 8 : l * 16 + 16] = jnp.broadcast_to(gain_grad, (8, channels))
        return (dy.astype(F32) + rstd[l] * inner).astype(BF16)

    dsend[...] = jnp.zeros(dsend.shape, F32)
    if half_rows * 2 > 5 * channels:
        part[...] = jnp.zeros(part.shape, F32)

    prepare(0, pair_ref)
    pl.semaphore_wait(barrier, n)
    start(0, bias_source(0), bias_target(0))
    project(0)
    finish(0, bias_source(0), bias_target(0))
    stack_bias(0)
    steps(0, rows, forward_row)
    asend_value = gate_output(0, pair_ref)
    turn_send(0, lambda a: asend_value[a * width : (a + 1) * width])
    dgated[...] = dot(cot_ref[...], wout_ref[1], 1, 1)
    turn_receive(0, x2)

    prepare(1, x2)
    start(1, bias_source(1), bias_target(1))
    project(1)
    finish(1, bias_source(1), bias_target(1))
    stack_bias(1)
    if not small:
        dacc[...] = jnp.zeros(dacc.shape, F32)
    steps(0, rows, functools.partial(backward_row, 1))
    send_bias_grad(1)
    out_ref[...] = gate_output(1, x2)
    dn = dot(dproj[...], wproj_ref[1], 1, 1)
    weight_grads(1, cot_ref[...])
    core_first(1).start()
    d_columns = layer_norm_grad(1, dn, cot_ref[...])
    turn_send(1, lambda a: d_columns[a * width : (a + 1) * width])
    core_sum(1)
    turn_receive(1, dy1)

    dgated[...] = dot(dy1[...], wout_ref[0], 1, 1)
    if not small:
        dacc[...] = jnp.zeros(dacc.shape, F32)
    steps(0, rows, functools.partial(backward_row, 0))
    send_bias_grad(0)
    axial_sum(1)
    weight_grads(0, dy1[...])
    core_first(0).start()
    dn = dot(dproj[...], wproj_ref[0], 1, 1)
    core_sum(0)
    grad_ref[...] = layer_norm_grad(0, dn, dy1[...])
    start(10, lambda peer: tails.at[me], lambda slot: tails.at[slot])
    axial_sum(0)
    finish(8 + 1, full_source(1), full_target(1))
    core_last(1).start()
    finish(10, lambda peer: tails.at[me], lambda slot: tails.at[slot])
    mine = jnp.sum(tails[...], axis=0)
    tail_ref[0] = mine
    core_copy(4, tail_ref.at[0], tail_ref.at[1]).start()
    finish(8, full_source(0), full_target(0))
    core_last(0).start()
    core_copy(4, tail_ref.at[0], tail_ref.at[1]).wait()
    tail_ref[0] = tail_ref[0] + tail_ref[1]
    for l in (1, 0):
        core_last_wait(l).wait()
        values = full[l].reshape(2 * half_rows, channels)
        for e in range(4):
            gproj_ref[l, :, e * channels : (e + 1) * channels] = values[e * channels : (e + 1) * channels]
        gout_ref[l] = values[4 * channels : 5 * channels]


def local(n, pair, pair_mask, ln_gain, projection_weight, pair_bias_weight, w_out, cotangent):
    rows, width, channels = pair.shape[1:]
    small = width <= 128
    slots = 2 if small else 1
    block = -(-rows * rows // 16) * 16
    chunk = -(-5 * channels // (2 * n * 8)) * 8
    wbias = jnp.pad(jnp.swapaxes(pair_bias_weight, 1, 2), ((0, 0), (0, 8 - H), (0, 0)))
    cot = jnp.swapaxes(cotangent[0], 0, 1).reshape(rows * width, channels)
    token = jnp.arange(width, dtype=jnp.int32)
    spread = ((token // rows) * block + (token % rows) * rows)[None, :]
    gather = ((token // rows) * block + token % rows)[:, None]
    size = rows * width
    shape = jax.ShapeDtypeStruct
    vmem = pltpu.VMEM
    whole = pl.BlockSpec(memory_space=pltpu.VMEM)
    out, grad, gproj, gout, tail = pl.pallas_call(
        functools.partial(kernel, n, rows, width, small, block, chunk),
        out_shape=(
            shape((size, channels), BF16),
            shape((size, channels), BF16),
            shape((2, channels, 4 * channels), F32),
            shape((2, channels, channels), F32),
            shape((2, 32, channels), F32),
        ),
        in_specs=[whole] * 9,
        out_specs=(whole,) * 5,
        scratch_shapes=[
            vmem((2, size, channels), F32),
            vmem((2, size, channels), F32),
            vmem((2, size, channels), BF16),
            vmem((2, size, 4 * channels), BF16),
            vmem((2, size, channels), F32),
            vmem((2, size, channels), F32),
            vmem((size, channels), F32),
            vmem((2, size, channels), BF16),
            vmem((size, 4 * channels), BF16),
            vmem((size, channels), BF16),
            vmem((size, channels), BF16),
            vmem((2, H * width, width), F32),
            vmem((H * width, width), F32),
            vmem((rows, H * width, width) if small else (1, 8, 128), F32),
            vmem((slots, width, 8, width), F32),
            vmem((slots, width, 8, width), F32),
            vmem((slots, n, rows, 8, width), F32),
            vmem((slots, n, block, channels), BF16),
            vmem((slots, n, block, channels), BF16),
            vmem((2, 2 * n * chunk, channels), F32),
            vmem((2, n * chunk, channels), F32),
            vmem((2, n, chunk, channels), F32),
            vmem((2, n, chunk, channels), F32),
            vmem((2, 2, n, chunk, channels), F32),
            vmem((n, 32, channels), F32),
            pltpu.SemaphoreType.DMA((11, n)),
            pltpu.SemaphoreType.DMA((11, n)),
            pltpu.SemaphoreType.DMA((5,)),
            pltpu.SemaphoreType.DMA((5,)),
        ],
        compiler_params=pltpu.CompilerParams(
            collective_id=0, has_side_effects=True, vmem_limit_bytes=(40 if small else 60) * 2**20
        ),
    )(pair.reshape(size, channels), pair_mask[0], ln_gain, projection_weight, wbias, w_out, cot, spread, gather)
    pair_out = jnp.swapaxes(out.reshape(rows, width, channels), 0, 1)[None]
    tail = tail[0].reshape(2, 16, channels)
    return (
        pair_out,
        grad.reshape(pair.shape),
        tail[:, 8],
        gproj,
        jnp.swapaxes(tail[:, :H], 1, 2),
        gout,
    )


def solution(mesh):
    placed = (
        P(("groups", "dp"), "axial", None, None),
        P(("groups", "dp"), "axial", None),
        P(),
        P(),
        P(),
        P(),
        P(("groups", "dp"), None, "axial", None),
    )
    return jax.shard_map(
        functools.partial(local, mesh.shape["axial"]),
        mesh=mesh,
        in_specs=placed,
        out_specs=(
            P(("groups", "dp"), None, "axial", None),
            P(("groups", "dp"), "axial", None, None),
            P("groups", None),
            P("groups", None, None),
            P("groups", None, None),
            P("groups", None, None),
        ),
        check_vma=False,
    )
```

```python
import functools
import math

import jax
import jax.numpy as jnp
from jax import lax
from jax.experimental import pallas as pl
from jax.experimental.pallas import tpu as pltpu
from jax.sharding import PartitionSpec as P

MESH = pl.DeviceIdType.MESH
F32, BF16 = jnp.float32, jnp.bfloat16
H = 4
EPS = 1e-05
MASKED = -1000000000.0
HIGHEST = lax.Precision.HIGHEST


def dot(a, b, ca, cb, precision=None):
    return lax.dot_general(a, b, (((ca,), (cb,)), ((), ())), precision=precision, preferred_element_type=F32)


def kernel(
    n, rows, width, small, block, chunk,
    pair_in, mask_in, gain_in, wproj_in, wbias_in, wout_in, cot_in,
    out_hbm, grad_hbm, gproj_hbm, gout_hbm, gbias_ref, ggain_ref,
    pair_ref, mask_ref, gain_ref, wproj_ref, wbias_raw, wbias_ref, wout_ref, cot_ref, out_ref, grad_ref, tail_ref,
    xhat, rstd, normed, proj, gate, att, dgated, gated, dproj, x2, dy1, bias, dacc, kept,
    bgat, dsend, drecv, asend, arecv, part, fromcore, half, red, full, tails,
    send_sem, recv_sem, core_send, core_recv, in_sem, out_sem,
):
    me = lax.axis_index("axial")
    core = lax.axis_index("dp")
    other = 1 - core
    channels = pair_ref.shape[1]
    head = channels // H
    scale = 1.0 / math.sqrt(head)
    stack = H if small else 1
    half_rows = n * chunk
    tight = width <= 64 and rows <= 8

    def slot_of(l):
        return l if small else 0

    def steps(low, high, body):
        if small:
            for idx in range(low, high):
                body(idx)
        else:
            lax.fori_loop(low, high, lambda idx, c: (body(idx), c)[1], 0)

    loads = [
        pltpu.make_async_copy(source, target, in_sem.at[idx])
        for idx, (source, target) in enumerate((
            (pair_in, pair_ref), (gain_in, gain_ref), (wbias_in, wbias_raw), (wproj_in, wproj_ref),
            (mask_in, mask_ref), (wout_in, wout_ref), (cot_in, cot_ref),
        ))
    ]
    for load in loads:
        load.start()

    barrier = pltpu.get_barrier_semaphore()

    def greet(off):
        pl.semaphore_signal(barrier, inc=1, device_id={"axial": lax.rem(me + off, n)}, device_id_type=MESH)

    steps(1, n, greet)
    pl.semaphore_signal(barrier, inc=1, device_id={"dp": other}, device_id_type=MESH)

    def axial_copy(phase, off, source, target, slot):
        peer = lax.rem(me + off, n)
        return pltpu.make_async_remote_copy(
            src_ref=source(peer), dst_ref=target(slot),
            send_sem=send_sem.at[phase, off], recv_sem=recv_sem.at[phase, off],
            device_id={"axial": peer}, device_id_type=MESH,
        )

    def start(phase, source, target):
        steps(1, n, lambda off: axial_copy(phase, off, source, target, me).start())

    def finish(phase, source, target):
        steps(1, n, lambda off: axial_copy(phase, off, source, target, lax.rem(me + n - off, n)).wait())

    def core_copy(phase, source, target):
        return pltpu.make_async_remote_copy(
            src_ref=source, dst_ref=target, send_sem=core_send.at[phase], recv_sem=core_recv.at[phase],
            device_id={"dp": other}, device_id_type=MESH,
        )

    def at_row(a):
        return pl.ds(a * width if small else pl.multiple_of(a * width, 16), width)

    def place(token, step):
        peer = ((token.astype(F32) + 0.5) * (1.0 / rows)).astype(jnp.int32)
        return peer * block + (token - peer * rows) * step

    spread = place(lax.broadcasted_iota(jnp.int32, (1, width), 1), rows)
    gather = place(lax.broadcasted_iota(jnp.int32, (width, 1), 0), 1)

    lanes = lax.broadcasted_iota(jnp.int32, (1, channels), 1)
    head_masks = [jnp.where((lanes >= h * head) & (lanes < (h + 1) * head), 1.0, 0.0) for h in range(H)]

    def packing(axis):
        shape = (width, n * 8) if axis == 0 else (n * 8, width)
        token = lax.broadcasted_iota(jnp.int32, (width, 1) if axis == 0 else (1, width), axis)
        peer = ((token.astype(F32) + 0.5) * (1.0 / rows)).astype(jnp.int32)
        spots = lax.broadcasted_iota(jnp.int32, shape, 1 - axis)
        return jnp.where(spots == token + peer * (8 - rows), 1.0, 0.0)

    def stacked(value, first):
        value = value.astype(F32)
        return jnp.concatenate([value * head_masks[first + h] for h in range(stack)], axis=0).astype(BF16)

    def merged(value, first):
        total = value[:width] * head_masks[first]
        for h in range(1, stack):
            total = total + value[h * width : (h + 1) * width] * head_masks[first + h]
        return total

    def prepare(l, x_ref):
        x = x_ref[...].astype(F32)
        centered = x - jnp.mean(x, axis=-1, keepdims=True)
        spread = lax.rsqrt(jnp.mean(centered * centered, axis=-1, keepdims=True) + EPS)
        hat = centered * spread
        xhat[l] = hat
        rstd[l] = jnp.broadcast_to(spread, hat.shape)
        normed[l] = (hat * gain_ref[l : l + 1]).astype(BF16)

        def own_bias(a):
            values = dot(wbias_ref[l], normed[l, at_row(a)], 1, 1)
            if tight:
                for h in range(H):
                    low = (h % 2) * 64
                    bgat[l, me, h // 2, a : a + 1, low : low + width] = values[h : h + 1]
            else:
                bgat[slot_of(l), me * rows + a] = values

        steps(0, rows, own_bias)

    def project(l):
        values = dot(normed[l], wproj_ref[l], 1, 0).astype(BF16)
        proj[l] = values
        gate[l] = jax.nn.sigmoid(values[:, 3 * channels :].astype(F32))

    def bias_source(l):
        return lambda peer: bgat.at[l, me] if tight else bgat.at[slot_of(l), pl.ds(me * rows, rows)]

    def bias_target(l):
        return lambda slot: bgat.at[l, slot] if tight else bgat.at[slot_of(l), pl.ds(slot * rows, rows)]

    def stack_bias(l):
        if tight:
            chosen = packing(0)
            for pair in range(H // 2):
                values = dot(chosen, bgat[l, :, pair].reshape(n * 8, 128), 1, 0, HIGHEST)
                for u in range(2):
                    first = (2 * pair + u) * width
                    bias[l, first : first + width] = values[:, u * 64 : u * 64 + width]
            return
        for h in range(H):
            bias[l, h * width : (h + 1) * width] = bgat[slot_of(l), :, h, :]

    def probabilities(l, a, first, queries, keys):
        scores = dot(queries, keys, 1, 1) * scale + bias[l, first * width : (first + stack) * width]
        scores = jnp.where(mask_ref[a] > 0, scores, MASKED)
        top = jnp.max(scores, axis=-1, keepdims=True)
        weights = jnp.exp(scores - top)
        return weights * (1.0 / jnp.sum(weights, axis=-1, keepdims=True))

    def column(l, a, part_index):
        return proj[l, at_row(a), part_index * channels : (part_index + 1) * channels]

    def forward_row(a):
        keys, values, query = column(0, a, 1), column(0, a, 2), column(0, a, 0)
        total = None
        for first in range(0, H, stack):
            probs = probabilities(0, a, first, stacked(query, first), keys)
            if small:
                kept[a] = probs
            term = merged(dot(probs.astype(BF16), values, 1, 0), first)
            total = term if total is None else total + term
        att[0, at_row(a)] = total

    def backward_row(l, a):
        keys, values, query = column(l, a, 1), column(l, a, 2), column(l, a, 0)
        gates = gate[l, at_row(a)]
        d_row = dgated[at_row(a)]
        d_att = (d_row * gates).astype(BF16)
        keep = mask_ref[a] > 0
        total = d_query = d_keys = d_values = None
        for first in range(0, H, stack):
            queries = stacked(query, first)
            probs = kept[a] if small and l == 0 else probabilities(l, a, first, queries, keys)
            probs_b = probs.astype(BF16)
            d_stack = stacked(d_att, first)
            if l == 1:
                term = merged(dot(probs_b, values, 1, 0), first)
                total = term if total is None else total + term
            d_probs = dot(d_stack, values, 1, 1)
            inner = jnp.sum(probs * d_probs, axis=-1, keepdims=True)
            d_scores = jnp.where(keep, probs * (d_probs - inner), 0.0)
            where = slice(first * width, (first + stack) * width)
            if small and a == 0:
                dacc[where] = d_scores
            else:
                dacc[where] += d_scores
            d_b = d_scores.astype(BF16)
            terms = (merged(dot(d_b, keys, 1, 0), first), dot(d_b, queries, 0, 0), dot(probs_b, d_stack, 0, 0))
            if d_query is None:
                d_query, d_keys, d_values = terms
            else:
                d_query, d_keys, d_values = d_query + terms[0], d_keys + terms[1], d_values + terms[2]
        if l == 1:
            att[1, at_row(a)] = total
        else:
            total = att[0, at_row(a)]
        d_gate = d_row * total * gates * (1.0 - gates)
        dproj[at_row(a), :channels] = (d_query * scale).astype(BF16)
        dproj[at_row(a), channels : 2 * channels] = (d_keys * scale).astype(BF16)
        dproj[at_row(a), 2 * channels : 3 * channels] = d_values.astype(BF16)
        dproj[at_row(a), 3 * channels :] = d_gate.astype(BF16)

    def gate_output(l, x_ref):
        values = (gate[l] * att[l]).astype(BF16)
        gated[l] = values
        return (x_ref[...].astype(F32) + dot(values, wout_ref[l], 1, 0)).astype(BF16)

    def turn_send(index, value_at):
        def turned(base, length):
            total = None
            for a in range(rows):
                spots = lax.broadcasted_iota(jnp.int32, (length, width), 0) + (base - a)
                chosen = jnp.where(spots == spread, 1.0, 0.0).astype(BF16)
                term = dot(chosen, value_at(a), 1, 0)
                total = term if total is None else total + term
            return total.astype(BF16)

        def one(peer):
            asend[slot_of(index), peer] = turned(peer * block, block)

        if small:
            asend[index] = turned(0, n * block).reshape(n, block, channels)
        else:
            steps(0, n, one)
        arecv[slot_of(index), me] = asend[slot_of(index), me]
        start(4 + index, lambda peer: asend.at[slot_of(index), peer], lambda slot: arecv.at[slot_of(index), slot])

    def turn_receive(index, target):
        finish(4 + index, lambda peer: asend.at[slot_of(index), peer], lambda slot: arecv.at[slot_of(index), slot])
        arrived = arecv[slot_of(index)].reshape(n * block, channels)

        def one(a):
            spots = lax.broadcasted_iota(jnp.int32, (width, n * block), 1) - a * rows
            chosen = jnp.where(spots == gather, 1.0, 0.0).astype(BF16)
            target[at_row(a)] = dot(chosen, arrived, 1, 0).astype(BF16)

        steps(0, rows, one)

    def ds_source(l):
        return lambda peer: dsend.at[l, peer] if tight else dsend.at[slot_of(l), pl.ds(peer * rows, rows)]

    def ds_target(l):
        return lambda slot: drecv.at[slot_of(l), slot]

    def send_bias_grad(l):
        if tight:
            chosen = packing(1)
            gap = jnp.zeros((width, 64 - width), F32)
            for pair in range(H // 2):
                first = 2 * pair * width
                both = [dacc[first : first + width], gap, dacc[first + width : first + 2 * width], gap]
                values = dot(chosen, jnp.concatenate(both, axis=1), 1, 0, HIGHEST)
                dsend[l, :, pair] = values.reshape(n, 8, 128)
            drecv[l, me] = dsend[l, me]
        else:
            for h in range(H):
                dsend[slot_of(l), :, h, :] = dacc[h * width : (h + 1) * width]
            drecv[slot_of(l), me] = dsend[slot_of(l), pl.ds(me * rows, rows)]
        start(2 + l, ds_source(l), ds_target(l))

    def weight_grads(l, dy):
        values = dot(normed[l], dproj[...], 0, 0)
        for e in range(4):
            part[l, e * channels : (e + 1) * channels] = values[:, e * channels : (e + 1) * channels]
        part[l, 4 * channels : 5 * channels] = dot(gated[l], dy, 0, 0)

    def core_first(l):
        return core_copy(l, part.at[l, pl.ds(other * half_rows, half_rows)], fromcore.at[l])

    def reduce_source(l):
        return lambda peer: half.at[l, peer]

    def reduce_target(l):
        return lambda slot: red.at[l, slot]

    def core_sum(l):
        core_first(l).wait()
        value = part[l, pl.ds(pl.multiple_of(core * half_rows, 8), half_rows)] + fromcore[l]
        half[l] = value.reshape(n, chunk, channels)
        red[l, me] = half[l, me]
        start(6 + l, reduce_source(l), reduce_target(l))

    def full_source(l):
        return lambda peer: full.at[l, chunk_at(me)]

    def full_target(l):
        return lambda slot: full.at[l, chunk_at(slot)]

    def chunk_at(slot):
        return pl.ds(pl.multiple_of((core * n + slot) * chunk, 8), chunk)

    def half_at(which):
        return pl.ds(pl.multiple_of(which * half_rows, 8), half_rows)

    def axial_sum(l):
        finish(6 + l, reduce_source(l), reduce_target(l))
        full[l, chunk_at(me)] = jnp.sum(red[l], axis=0)
        start(8 + l, full_source(l), full_target(l))

    def core_last(l):
        return core_copy(2 + l, full.at[l, half_at(core)], full.at[l, half_at(core)])

    def core_last_wait(l):
        return core_copy(2 + l, full.at[l, half_at(core)], full.at[l, half_at(other)])

    def layer_norm_grad(l, dn, dy):
        finish(2 + l, ds_source(l), ds_target(l))
        own = jnp.sum(drecv[slot_of(l)], axis=0)
        if tight:
            spare = jnp.zeros((8 - H, width), F32)
            own = [
                jnp.concatenate(
                    [own[h // 2, a : a + 1, (h % 2) * 64 : (h % 2) * 64 + width] for h in range(H)] + [spare], axis=0
                )
                for a in range(rows)
            ]
        extra, bias_grad = [], None
        weights = wbias_ref[l].astype(F32)
        for a in range(rows):
            extra.append(dot(own[a], weights, 0, 0, HIGHEST))
            term = dot(own[a], normed[l, a * width : (a + 1) * width].astype(F32), 1, 0, HIGHEST)
            bias_grad = term if bias_grad is None else bias_grad + term
        dn = dn + jnp.concatenate(extra, axis=0)
        hat = xhat[l]
        gain_grad = jnp.sum(dn * hat, axis=0, keepdims=True)
        d_hat = dn * gain_ref[l : l + 1]
        inner = (
            d_hat
            - jnp.mean(d_hat, axis=-1, keepdims=True)
            - hat * jnp.mean(d_hat * hat, axis=-1, keepdims=True)
        )
        tails[me, l * 8 : l * 8 + H] = bias_grad[:H]
        tails[me, l * 8 + H : l * 8 + 8] = jnp.broadcast_to(gain_grad, (8 - H, channels))
        return (dy.astype(F32) + rstd[l] * inner).astype(BF16)

    stores = []

    def store(idx, source, target):
        stores.append(pltpu.make_async_copy(source, target, out_sem.at[idx]))
        stores[-1].start()

    if tight:
        bgat[:, me] = jnp.zeros((2,) + bgat.shape[2:], F32)
    else:
        dsend[...] = jnp.zeros(dsend.shape, F32)
    if half_rows * 2 > 5 * channels:
        part[...] = jnp.zeros(part.shape, F32)

    for load in loads[:3]:
        load.wait()
    for l in range(2):
        spare = jnp.zeros((8 - H, channels), F32)
        wbias_ref[l] = jnp.concatenate([wbias_raw[l].astype(F32), spare], axis=0).astype(BF16)
    prepare(0, pair_ref)
    pl.semaphore_wait(barrier, n)
    start(0, bias_source(0), bias_target(0))
    loads[3].wait()
    project(0)
    finish(0, bias_source(0), bias_target(0))
    stack_bias(0)
    for load in loads[4:]:
        load.wait()
    steps(0, rows, forward_row)
    asend_value = gate_output(0, pair_ref)
    turn_send(0, lambda a: asend_value[a * width : (a + 1) * width])
    dgated[...] = dot(cot_ref[...], wout_ref[1], 1, 1)
    turn_receive(0, x2)

    prepare(1, x2)
    start(1, bias_source(1), bias_target(1))
    project(1)
    finish(1, bias_source(1), bias_target(1))
    stack_bias(1)
    if not small:
        dacc[...] = jnp.zeros(dacc.shape, F32)
    steps(0, rows, functools.partial(backward_row, 1))
    send_bias_grad(1)
    out_ref[...] = gate_output(1, x2)
    store(0, out_ref, out_hbm)
    dn = dot(dproj[...], wproj_ref[1], 1, 1)
    weight_grads(1, cot_ref[...])
    core_first(1).start()
    d_columns = layer_norm_grad(1, dn, cot_ref[...])
    turn_send(1, lambda a: d_columns[a * width : (a + 1) * width])
    core_sum(1)
    turn_receive(1, dy1)

    dgated[...] = dot(dy1[...], wout_ref[0], 1, 1)
    if not small:
        dacc[...] = jnp.zeros(dacc.shape, F32)
    steps(0, rows, functools.partial(backward_row, 0))
    send_bias_grad(0)
    axial_sum(1)
    weight_grads(0, dy1[...])
    core_first(0).start()
    dn = dot(dproj[...], wproj_ref[0], 1, 1)
    core_sum(0)
    grad_ref[...] = layer_norm_grad(0, dn, dy1[...])
    store(1, grad_ref, grad_hbm)
    start(10, lambda peer: tails.at[me], lambda slot: tails.at[slot])
    axial_sum(0)
    finish(8 + 1, full_source(1), full_target(1))
    core_last(1).start()
    finish(10, lambda peer: tails.at[me], lambda slot: tails.at[slot])
    mine = jnp.sum(tails[...], axis=0)
    tail_ref[0] = mine
    core_copy(4, tail_ref.at[0], tail_ref.at[1]).start()
    finish(8, full_source(0), full_target(0))
    core_last(0).start()
    core_copy(4, tail_ref.at[0], tail_ref.at[1]).wait()
    tail_ref[0] = tail_ref[0] + tail_ref[1]
    for l in range(2):
        gbias_ref[l] = tail_ref[0, l * 8 : l * 8 + H]
        ggain_ref[l : l + 1] = tail_ref[0, l * 8 + H : l * 8 + H + 1]
    for l in (1, 0):
        core_last_wait(l).wait()
        for e in range(4):
            store(
                2 + 5 * l + e, full.at[l, pl.ds(e * channels, channels)],
                gproj_hbm.at[l, :, pl.ds(e * channels, channels)],
            )
        store(6 + 5 * l, full.at[l, pl.ds(4 * channels, channels)], gout_hbm.at[l])
    for copy in stores:
        copy.wait()


def hand_over(*refs):
    copies = [pltpu.make_async_copy(refs[idx], refs[6 + idx], refs[12].at[idx]) for idx in range(6)]
    for copy in copies:
        copy.start()
    for copy in copies:
        copy.wait()


def local(n, pair, pair_mask, ln_gain, projection_weight, pair_bias_weight, w_out, cotangent):
    rows, width, channels = pair.shape[1:]
    small = width <= 128
    slots = 2 if small else 1
    tight = width <= 64 and rows <= 8
    block = -(-rows * rows // 16) * 16
    chunk = -(-5 * channels // (2 * n * 8)) * 8
    wbias = jnp.swapaxes(pair_bias_weight, 1, 2)
    cot = jnp.swapaxes(cotangent[0], 0, 1).reshape(rows * width, channels)
    size = rows * width
    shape = jax.ShapeDtypeStruct
    vmem = pltpu.VMEM
    whole = pl.BlockSpec(memory_space=pltpu.VMEM)
    hbm = pl.BlockSpec(memory_space=pltpu.HBM)
    results = (
        shape((size, channels), BF16),
        shape((size, channels), BF16),
        shape((2, channels, 4 * channels), F32),
        shape((2, channels, channels), F32),
        shape((2, H, channels), F32),
        shape((2, channels), F32),
    )
    made = pl.pallas_call(
        functools.partial(kernel, n, rows, width, small, block, chunk),
        out_shape=results,
        in_specs=[hbm] * 7,
        out_specs=(hbm,) * 4 + (whole,) * 2,
        scratch_shapes=[
            vmem((size, channels), BF16),
            vmem((rows, 1, width), jnp.int32),
            vmem((2, channels), F32),
            vmem((2, channels, 4 * channels), BF16),
            vmem((2, H, channels), BF16),
            vmem((2, 8, channels), BF16),
            vmem((2, channels, channels), BF16),
            vmem((size, channels), BF16),
            vmem((size, channels), BF16),
            vmem((size, channels), BF16),
            vmem((2, 16, channels), F32),
            vmem((2, size, channels), F32),
            vmem((2, size, channels), F32),
            vmem((2, size, channels), BF16),
            vmem((2, size, 4 * channels), BF16),
            vmem((2, size, channels), F32),
            vmem((2, size, channels), F32),
            vmem((size, channels), F32),
            vmem((2, size, channels), BF16),
            vmem((size, 4 * channels), BF16),
            vmem((size, channels), BF16),
            vmem((size, channels), BF16),
            vmem((2, H * width, width), F32),
            vmem((H * width, width), F32),
            vmem((rows, H * width, width) if small else (1, 8, 128), F32),
            vmem((2, n, 2, 8, 128) if tight else (slots, width, 8, width), F32),
            vmem((2, n, 2, 8, 128) if tight else (slots, width, 8, width), F32),
            vmem((2, n, 2, 8, 128) if tight else (slots, n, rows, 8, width), F32),
            vmem((slots, n, block, channels), BF16),
            vmem((slots, n, block, channels), BF16),
            vmem((2, 2 * n * chunk, channels), F32),
            vmem((2, n * chunk, channels), F32),
            vmem((2, n, chunk, channels), F32),
            vmem((2, n, chunk, channels), F32),
            vmem((2, 2 * n * chunk, channels), F32),
            vmem((n, 16, channels), F32),
            pltpu.SemaphoreType.DMA((11, n)),
            pltpu.SemaphoreType.DMA((11, n)),
            pltpu.SemaphoreType.DMA((5,)),
            pltpu.SemaphoreType.DMA((5,)),
            pltpu.SemaphoreType.DMA((7,)),
            pltpu.SemaphoreType.DMA((12,)),
        ],
        compiler_params=pltpu.CompilerParams(
            collective_id=0, has_side_effects=True, vmem_limit_bytes=63 * 2**20
        ),
    )(pair.reshape(size, channels), pair_mask.reshape(rows, 1, width), ln_gain, projection_weight, wbias, w_out, cot)
    out, grad, gproj, gout, gbias, ggain = pl.pallas_call(
        hand_over,
        out_shape=results,
        in_specs=[hbm] * 6,
        out_specs=(hbm,) * 6,
        scratch_shapes=[pltpu.SemaphoreType.DMA((6,))],
        compiler_params=pltpu.CompilerParams(vmem_limit_bytes=63 * 2**20),
    )(*made)
    return (
        jnp.swapaxes(out.reshape(rows, width, channels), 0, 1)[None],
        grad.reshape(pair.shape),
        ggain,
        gproj,
        jnp.swapaxes(gbias, 1, 2),
        gout,
    )


def solution(mesh):
    placed = (
        P(("groups", "dp"), "axial", None, None),
        P(("groups", "dp"), "axial", None),
        P(),
        P(),
        P(),
        P(),
        P(("groups", "dp"), None, "axial", None),
    )
    return jax.shard_map(
        functools.partial(local, mesh.shape["axial"]),
        mesh=mesh,
        in_specs=placed,
        out_specs=(
            P(("groups", "dp"), None, "axial", None),
            P(("groups", "dp"), "axial", None, None),
            P("groups", None),
            P("groups", None, None),
            P("groups", None, None),
            P("groups", None, None),
        ),
        check_vma=False,
    )
```

```python
import functools
import math

import jax
import jax.numpy as jnp
from jax import lax
from jax.experimental import pallas as pl
from jax.experimental.pallas import tpu as pltpu
from jax.sharding import PartitionSpec as P

MESH = pl.DeviceIdType.MESH
F32, BF16 = jnp.float32, jnp.bfloat16
H = 4
EPS = 1e-05
MASKED = -1000000000.0
HIGHEST = lax.Precision.HIGHEST


def dot(a, b, ca, cb, precision=None):
    return lax.dot_general(a, b, (((ca,), (cb,)), ((), ())), precision=precision, preferred_element_type=F32)


def kernel(
    n, rows, width, small, block, chunk,
    pair_in, mask_in, gain_in, wproj_in, wbias_in, wout_in, cot_in,
    out_hbm, grad_hbm, gproj_hbm, gout_hbm, gbias_ref, ggain_ref,
    pair_ref, mask_ref, gain_ref, wproj_ref, wbias_raw, wbias_ref, wout_ref, cot_ref, out_ref, grad_ref, tail_ref,
    xhat, rstd, normed, proj, gate, att, dgated, gated, dproj, x2, dy1, bias, dacc, kept,
    bgat, dsend, drecv, asend, arecv, part, fromcore, half, red, full, tails,
    send_sem, recv_sem, core_send, core_recv, in_sem, out_sem,
):
    me = lax.axis_index("axial")
    core = lax.axis_index("dp")
    other = 1 - core
    channels = pair_ref.shape[1]
    head = channels // H
    scale = 1.0 / math.sqrt(head)
    stack = H if small else 1
    half_rows = n * chunk
    tight = width <= 64 and rows <= 8

    def slot_of(l):
        return l if small else 0

    def steps(low, high, body):
        if small:
            for idx in range(low, high):
                body(idx)
        else:
            lax.fori_loop(low, high, lambda idx, c: (body(idx), c)[1], 0)

    loads = [
        pltpu.make_async_copy(source, target, in_sem.at[idx])
        for idx, (source, target) in enumerate((
            (pair_in, pair_ref), (gain_in, gain_ref), (wbias_in, wbias_raw), (wproj_in, wproj_ref),
            (mask_in, mask_ref), (wout_in, wout_ref), (cot_in, cot_ref),
        ))
    ]
    for load in loads:
        load.start()

    barrier = pltpu.get_barrier_semaphore()

    def greet(off):
        pl.semaphore_signal(barrier, inc=1, device_id={"axial": lax.rem(me + off, n)}, device_id_type=MESH)

    steps(1, n, greet)
    pl.semaphore_signal(barrier, inc=1, device_id={"dp": other}, device_id_type=MESH)

    def axial_copy(phase, off, source, target, slot):
        peer = lax.rem(me + off, n)
        return pltpu.make_async_remote_copy(
            src_ref=source(peer), dst_ref=target(slot),
            send_sem=send_sem.at[phase, off], recv_sem=recv_sem.at[phase, off],
            device_id={"axial": peer}, device_id_type=MESH,
        )

    def start(phase, source, target):
        steps(1, n, lambda off: axial_copy(phase, off, source, target, me).start())

    def finish(phase, source, target):
        steps(1, n, lambda off: axial_copy(phase, off, source, target, lax.rem(me + n - off, n)).wait())

    def core_copy(phase, source, target):
        return pltpu.make_async_remote_copy(
            src_ref=source, dst_ref=target, send_sem=core_send.at[phase], recv_sem=core_recv.at[phase],
            device_id={"dp": other}, device_id_type=MESH,
        )

    def at_row(a):
        return pl.ds(a * width if small else pl.multiple_of(a * width, 16), width)

    def place(token, step):
        peer = ((token.astype(F32) + 0.5) * (1.0 / rows)).astype(jnp.int32)
        return peer * block + (token - peer * rows) * step

    spread = place(lax.broadcasted_iota(jnp.int32, (1, width), 1), rows)
    gather = place(lax.broadcasted_iota(jnp.int32, (width, 1), 0), 1)

    lanes = lax.broadcasted_iota(jnp.int32, (1, channels), 1)
    head_masks = [jnp.where((lanes >= h * head) & (lanes < (h + 1) * head), 1.0, 0.0) for h in range(H)]

    def packing(axis):
        shape = (width, n * 8) if axis == 0 else (n * 8, width)
        token = lax.broadcasted_iota(jnp.int32, (width, 1) if axis == 0 else (1, width), axis)
        peer = ((token.astype(F32) + 0.5) * (1.0 / rows)).astype(jnp.int32)
        spots = lax.broadcasted_iota(jnp.int32, shape, 1 - axis)
        return jnp.where(spots == token + peer * (8 - rows), 1.0, 0.0)

    def stacked(value, first):
        value = value.astype(F32)
        return jnp.concatenate([value * head_masks[first + h] for h in range(stack)], axis=0).astype(BF16)

    def merged(value, first):
        total = value[:width] * head_masks[first]
        for h in range(1, stack):
            total = total + value[h * width : (h + 1) * width] * head_masks[first + h]
        return total

    def prepare(l, x_ref):
        x = x_ref[...].astype(F32)
        centered = x - jnp.mean(x, axis=-1, keepdims=True)
        spread = lax.rsqrt(jnp.mean(centered * centered, axis=-1, keepdims=True) + EPS)
        hat = centered * spread
        xhat[l] = hat
        rstd[l] = jnp.broadcast_to(spread, hat.shape)
        normed[l] = (hat * gain_ref[l : l + 1]).astype(BF16)

        def own_bias(a):
            values = dot(wbias_ref[l], normed[l, at_row(a)], 1, 1)
            if tight:
                for h in range(H):
                    low = (h % 2) * 64
                    bgat[l, me, h // 2, a : a + 1, low : low + width] = values[h : h + 1]
            else:
                bgat[slot_of(l), me * rows + a] = values

        steps(0, rows, own_bias)

    def project(l):
        values = dot(normed[l], wproj_ref[l], 1, 0).astype(BF16)
        proj[l] = values
        gate[l] = jax.nn.sigmoid(values[:, 3 * channels :].astype(F32))

    def bias_source(l):
        return lambda peer: bgat.at[l, me] if tight else bgat.at[slot_of(l), pl.ds(me * rows, rows)]

    def bias_target(l):
        return lambda slot: bgat.at[l, slot] if tight else bgat.at[slot_of(l), pl.ds(slot * rows, rows)]

    def stack_bias(l):
        if tight:
            chosen = packing(0)
            for pair in range(H // 2):
                values = dot(chosen, bgat[l, :, pair].reshape(n * 8, 128), 1, 0, HIGHEST)
                for u in range(2):
                    first = (2 * pair + u) * width
                    bias[l, first : first + width] = values[:, u * 64 : u * 64 + width]
            return
        for h in range(H):
            bias[l, h * width : (h + 1) * width] = bgat[slot_of(l), :, h, :]

    def probabilities(l, a, first, queries, keys):
        scores = dot(queries, keys, 1, 1) * scale + bias[l, first * width : (first + stack) * width]
        scores = jnp.where(mask_ref[a] > 0, scores, MASKED)
        top = jnp.max(scores, axis=-1, keepdims=True)
        weights = jnp.exp(scores - top)
        return weights * (1.0 / jnp.sum(weights, axis=-1, keepdims=True))

    def column(l, a, part_index):
        return proj[l, at_row(a), part_index * channels : (part_index + 1) * channels]

    def forward_row(a):
        keys, values, query = column(0, a, 1), column(0, a, 2), column(0, a, 0)
        total = None
        for first in range(0, H, stack):
            probs = probabilities(0, a, first, stacked(query, first), keys)
            if small:
                kept[a] = probs
            term = merged(dot(probs.astype(BF16), values, 1, 0), first)
            total = term if total is None else total + term
        att[0, at_row(a)] = total

    def backward_row(l, a):
        keys, values, query = column(l, a, 1), column(l, a, 2), column(l, a, 0)
        gates = gate[l, at_row(a)]
        d_row = dgated[at_row(a)]
        d_att = (d_row * gates).astype(BF16)
        keep = mask_ref[a] > 0
        total = d_query = d_keys = d_values = None
        for first in range(0, H, stack):
            queries = stacked(query, first)
            probs = kept[a] if small and l == 0 else probabilities(l, a, first, queries, keys)
            probs_b = probs.astype(BF16)
            d_stack = stacked(d_att, first)
            if l == 1:
                term = merged(dot(probs_b, values, 1, 0), first)
                total = term if total is None else total + term
            d_probs = dot(d_stack, values, 1, 1)
            inner = jnp.sum(probs * d_probs, axis=-1, keepdims=True)
            d_scores = jnp.where(keep, probs * (d_probs - inner), 0.0)
            where = slice(first * width, (first + stack) * width)
            if small and a == 0:
                dacc[where] = d_scores
            else:
                dacc[where] += d_scores
            d_b = d_scores.astype(BF16)
            terms = (merged(dot(d_b, keys, 1, 0), first), dot(d_b, queries, 0, 0), dot(probs_b, d_stack, 0, 0))
            if d_query is None:
                d_query, d_keys, d_values = terms
            else:
                d_query, d_keys, d_values = d_query + terms[0], d_keys + terms[1], d_values + terms[2]
        if l == 1:
            att[1, at_row(a)] = total
        else:
            total = att[0, at_row(a)]
        d_gate = d_row * total * gates * (1.0 - gates)
        dproj[at_row(a), :channels] = (d_query * scale).astype(BF16)
        dproj[at_row(a), channels : 2 * channels] = (d_keys * scale).astype(BF16)
        dproj[at_row(a), 2 * channels : 3 * channels] = d_values.astype(BF16)
        dproj[at_row(a), 3 * channels :] = d_gate.astype(BF16)

    def gate_output(l, x_ref):
        values = (gate[l] * att[l]).astype(BF16)
        gated[l] = values
        return (x_ref[...].astype(F32) + dot(values, wout_ref[l], 1, 0)).astype(BF16)

    def turn_send(index, value_at):
        def turned(base, length):
            total = None
            for a in range(rows):
                spots = lax.broadcasted_iota(jnp.int32, (length, width), 0) + (base - a)
                chosen = jnp.where(spots == spread, 1.0, 0.0).astype(BF16)
                term = dot(chosen, value_at(a), 1, 0)
                total = term if total is None else total + term
            return total.astype(BF16)

        def one(peer):
            asend[slot_of(index), peer] = turned(peer * block, block)

        if small:
            asend[index] = turned(0, n * block).reshape(n, block, channels)
        else:
            steps(0, n, one)
        arecv[slot_of(index), me] = asend[slot_of(index), me]
        start(4 + index, lambda peer: asend.at[slot_of(index), peer], lambda slot: arecv.at[slot_of(index), slot])

    def turn_receive(index, target):
        finish(4 + index, lambda peer: asend.at[slot_of(index), peer], lambda slot: arecv.at[slot_of(index), slot])
        arrived = arecv[slot_of(index)].reshape(n * block, channels)

        def one(a):
            spots = lax.broadcasted_iota(jnp.int32, (width, n * block), 1) - a * rows
            chosen = jnp.where(spots == gather, 1.0, 0.0).astype(BF16)
            target[at_row(a)] = dot(chosen, arrived, 1, 0).astype(BF16)

        steps(0, rows, one)

    def ds_source(l):
        return lambda peer: dsend.at[l, peer] if tight else dsend.at[slot_of(l), pl.ds(peer * rows, rows)]

    def ds_target(l):
        return lambda slot: drecv.at[slot_of(l), slot]

    def send_bias_grad(l):
        if tight:
            chosen = packing(1)
            gap = jnp.zeros((width, 64 - width), F32)
            for pair in range(H // 2):
                first = 2 * pair * width
                both = [dacc[first : first + width], gap, dacc[first + width : first + 2 * width], gap]
                values = dot(chosen, jnp.concatenate(both, axis=1), 1, 0, HIGHEST)
                dsend[l, :, pair] = values.reshape(n, 8, 128)
            drecv[l, me] = dsend[l, me]
        else:
            for h in range(H):
                dsend[slot_of(l), :, h, :] = dacc[h * width : (h + 1) * width]
            drecv[slot_of(l), me] = dsend[slot_of(l), pl.ds(me * rows, rows)]
        start(2 + l, ds_source(l), ds_target(l))

    def weight_grads(l, dy):
        values = dot(normed[l], dproj[...], 0, 0)
        for e in range(4):
            part[l, e * channels : (e + 1) * channels] = values[:, e * channels : (e + 1) * channels]
        part[l, 4 * channels : 5 * channels] = dot(gated[l], dy, 0, 0)

    def core_first(l):
        return core_copy(l, part.at[l, pl.ds(other * half_rows, half_rows)], fromcore.at[l])

    def reduce_source(l):
        return lambda peer: half.at[l, peer]

    def reduce_target(l):
        return lambda slot: red.at[l, slot]

    def core_sum(l):
        core_first(l).wait()
        value = part[l, pl.ds(pl.multiple_of(core * half_rows, 8), half_rows)] + fromcore[l]
        half[l] = value.reshape(n, chunk, channels)
        red[l, me] = half[l, me]
        start(6 + l, reduce_source(l), reduce_target(l))

    def full_source(l):
        return lambda peer: full.at[l, chunk_at(me)]

    def full_target(l):
        return lambda slot: full.at[l, chunk_at(slot)]

    def chunk_at(slot):
        return pl.ds(pl.multiple_of((core * n + slot) * chunk, 8), chunk)

    def half_at(which):
        return pl.ds(pl.multiple_of(which * half_rows, 8), half_rows)

    def axial_sum(l):
        finish(6 + l, reduce_source(l), reduce_target(l))
        full[l, chunk_at(me)] = jnp.sum(red[l], axis=0)
        start(8 + l, full_source(l), full_target(l))

    def core_last(l):
        return core_copy(2 + l, full.at[l, half_at(core)], full.at[l, half_at(core)])

    def core_last_wait(l):
        return core_copy(2 + l, full.at[l, half_at(core)], full.at[l, half_at(other)])

    def layer_norm_grad(l, dn, dy):
        finish(2 + l, ds_source(l), ds_target(l))
        own = jnp.sum(drecv[slot_of(l)], axis=0)
        if tight:
            spare = jnp.zeros((8 - H, width), F32)
            own = [
                jnp.concatenate(
                    [own[h // 2, a : a + 1, (h % 2) * 64 : (h % 2) * 64 + width] for h in range(H)] + [spare], axis=0
                )
                for a in range(rows)
            ]
        extra, bias_grad = [], None
        weights = wbias_ref[l].astype(F32)
        for a in range(rows):
            extra.append(dot(own[a], weights, 0, 0, HIGHEST))
            term = dot(own[a], normed[l, a * width : (a + 1) * width].astype(F32), 1, 0, HIGHEST)
            bias_grad = term if bias_grad is None else bias_grad + term
        dn = dn + jnp.concatenate(extra, axis=0)
        hat = xhat[l]
        gain_grad = jnp.sum(dn * hat, axis=0, keepdims=True)
        d_hat = dn * gain_ref[l : l + 1]
        inner = (
            d_hat
            - jnp.mean(d_hat, axis=-1, keepdims=True)
            - hat * jnp.mean(d_hat * hat, axis=-1, keepdims=True)
        )
        tails[me, l * 8 : l * 8 + H] = bias_grad[:H]
        tails[me, l * 8 + H : l * 8 + 8] = jnp.broadcast_to(gain_grad, (8 - H, channels))
        return (dy.astype(F32) + rstd[l] * inner).astype(BF16)

    stores = []

    def store(idx, source, target):
        stores.append(pltpu.make_async_copy(source, target, out_sem.at[idx]))
        stores[-1].start()

    if tight:
        bgat[:, me] = jnp.zeros((2,) + bgat.shape[2:], F32)
    else:
        dsend[...] = jnp.zeros(dsend.shape, F32)
    if half_rows * 2 > 5 * channels:
        part[...] = jnp.zeros(part.shape, F32)

    for load in loads[:3]:
        load.wait()
    for l in range(2):
        spare = jnp.zeros((8 - H, channels), F32)
        wbias_ref[l] = jnp.concatenate([wbias_raw[l].astype(F32), spare], axis=0).astype(BF16)
    prepare(0, pair_ref)
    pl.semaphore_wait(barrier, n)
    start(0, bias_source(0), bias_target(0))
    loads[3].wait()
    project(0)
    finish(0, bias_source(0), bias_target(0))
    stack_bias(0)
    for load in loads[4:]:
        load.wait()
    steps(0, rows, forward_row)
    asend_value = gate_output(0, pair_ref)
    turn_send(0, lambda a: asend_value[a * width : (a + 1) * width])
    dgated[...] = dot(cot_ref[...], wout_ref[1], 1, 1)
    turn_receive(0, x2)

    prepare(1, x2)
    start(1, bias_source(1), bias_target(1))
    project(1)
    finish(1, bias_source(1), bias_target(1))
    stack_bias(1)
    if not small:
        dacc[...] = jnp.zeros(dacc.shape, F32)
    steps(0, rows, functools.partial(backward_row, 1))
    send_bias_grad(1)
    out_ref[...] = gate_output(1, x2)
    store(0, out_ref, out_hbm)
    dn = dot(dproj[...], wproj_ref[1], 1, 1)
    weight_grads(1, cot_ref[...])
    core_first(1).start()
    d_columns = layer_norm_grad(1, dn, cot_ref[...])
    turn_send(1, lambda a: d_columns[a * width : (a + 1) * width])
    core_sum(1)
    turn_receive(1, dy1)

    dgated[...] = dot(dy1[...], wout_ref[0], 1, 1)
    if not small:
        dacc[...] = jnp.zeros(dacc.shape, F32)
    steps(0, rows // 2, functools.partial(backward_row, 0))
    axial_sum(1)
    steps(rows // 2, rows, functools.partial(backward_row, 0))
    send_bias_grad(0)
    weight_grads(0, dy1[...])
    core_first(0).start()
    dn = dot(dproj[...], wproj_ref[0], 1, 1)
    core_sum(0)
    grad_ref[...] = layer_norm_grad(0, dn, dy1[...])
    store(1, grad_ref, grad_hbm)
    start(10, lambda peer: tails.at[me], lambda slot: tails.at[slot])
    axial_sum(0)
    finish(8 + 1, full_source(1), full_target(1))
    core_last(1).start()
    finish(10, lambda peer: tails.at[me], lambda slot: tails.at[slot])
    mine = jnp.sum(tails[...], axis=0)
    tail_ref[0] = mine
    core_copy(4, tail_ref.at[0], tail_ref.at[1]).start()
    finish(8, full_source(0), full_target(0))
    core_last(0).start()
    core_copy(4, tail_ref.at[0], tail_ref.at[1]).wait()
    tail_ref[0] = tail_ref[0] + tail_ref[1]
    for l in range(2):
        gbias_ref[l] = tail_ref[0, l * 8 : l * 8 + H]
        ggain_ref[l : l + 1] = tail_ref[0, l * 8 + H : l * 8 + H + 1]
    for l in (1, 0):
        core_last_wait(l).wait()
        for e in range(4):
            store(
                2 + 5 * l + e, full.at[l, pl.ds(e * channels, channels)],
                gproj_hbm.at[l, :, pl.ds(e * channels, channels)],
            )
        store(6 + 5 * l, full.at[l, pl.ds(4 * channels, channels)], gout_hbm.at[l])
    for copy in stores:
        copy.wait()


def hand_over(*refs):
    sources, targets, held, semaphore = refs[:6], refs[6:12], refs[12:18], refs[18]
    inward = [pltpu.make_async_copy(sources[idx], held[idx], semaphore.at[0, idx]) for idx in range(6)]
    outward = [pltpu.make_async_copy(held[idx], targets[idx], semaphore.at[1, idx]) for idx in range(6)]
    for copy in inward:
        copy.start()
    for idx in range(6):
        inward[idx].wait()
        outward[idx].start()
    for copy in outward:
        copy.wait()


def local(n, pair, pair_mask, ln_gain, projection_weight, pair_bias_weight, w_out, cotangent):
    rows, width, channels = pair.shape[1:]
    small = width <= 128
    slots = 2 if small else 1
    tight = width <= 64 and rows <= 8
    block = -(-rows * rows // 16) * 16
    chunk = -(-5 * channels // (2 * n * 8)) * 8
    wbias = jnp.swapaxes(pair_bias_weight, 1, 2)
    cot = jnp.swapaxes(cotangent[0], 0, 1).reshape(rows * width, channels)
    size = rows * width
    shape = jax.ShapeDtypeStruct
    vmem = pltpu.VMEM
    whole = pl.BlockSpec(memory_space=pltpu.VMEM)
    hbm = pl.BlockSpec(memory_space=pltpu.HBM)
    results = (
        shape((size, channels), BF16),
        shape((size, channels), BF16),
        shape((2, channels, 4 * channels), F32),
        shape((2, channels, channels), F32),
        shape((2, H, channels), F32),
        shape((2, channels), F32),
    )
    made = pl.pallas_call(
        functools.partial(kernel, n, rows, width, small, block, chunk),
        out_shape=results,
        in_specs=[hbm] * 7,
        out_specs=(hbm,) * 4 + (whole,) * 2,
        scratch_shapes=[
            vmem((size, channels), BF16),
            vmem((rows, 1, width), jnp.int32),
            vmem((2, channels), F32),
            vmem((2, channels, 4 * channels), BF16),
            vmem((2, H, channels), BF16),
            vmem((2, 8, channels), BF16),
            vmem((2, channels, channels), BF16),
            vmem((size, channels), BF16),
            vmem((size, channels), BF16),
            vmem((size, channels), BF16),
            vmem((2, 16, channels), F32),
            vmem((2, size, channels), F32),
            vmem((2, size, channels), F32),
            vmem((2, size, channels), BF16),
            vmem((2, size, 4 * channels), BF16),
            vmem((2, size, channels), F32),
            vmem((2, size, channels), F32),
            vmem((size, channels), F32),
            vmem((2, size, channels), BF16),
            vmem((size, 4 * channels), BF16),
            vmem((size, channels), BF16),
            vmem((size, channels), BF16),
            vmem((2, H * width, width), F32),
            vmem((H * width, width), F32),
            vmem((rows, H * width, width) if small else (1, 8, 128), F32),
            vmem((2, n, 2, 8, 128) if tight else (slots, width, 8, width), F32),
            vmem((2, n, 2, 8, 128) if tight else (slots, width, 8, width), F32),
            vmem((2, n, 2, 8, 128) if tight else (slots, n, rows, 8, width), F32),
            vmem((slots, n, block, channels), BF16),
            vmem((slots, n, block, channels), BF16),
            vmem((2, 2 * n * chunk, channels), F32),
            vmem((2, n * chunk, channels), F32),
            vmem((2, n, chunk, channels), F32),
            vmem((2, n, chunk, channels), F32),
            vmem((2, 2 * n * chunk, channels), F32),
            vmem((n, 16, channels), F32),
            pltpu.SemaphoreType.DMA((11, n)),
            pltpu.SemaphoreType.DMA((11, n)),
            pltpu.SemaphoreType.DMA((5,)),
            pltpu.SemaphoreType.DMA((5,)),
            pltpu.SemaphoreType.DMA((7,)),
            pltpu.SemaphoreType.DMA((12,)),
        ],
        compiler_params=pltpu.CompilerParams(
            collective_id=0, has_side_effects=True, vmem_limit_bytes=63 * 2**20
        ),
    )(pair.reshape(size, channels), pair_mask.reshape(rows, 1, width), ln_gain, projection_weight, wbias, w_out, cot)
    out, grad, gproj, gout, gbias, ggain = pl.pallas_call(
        hand_over,
        out_shape=results,
        in_specs=[hbm] * 6,
        out_specs=(hbm,) * 6,
        scratch_shapes=[vmem(item.shape, item.dtype) for item in results] + [pltpu.SemaphoreType.DMA((2, 6))],
        compiler_params=pltpu.CompilerParams(vmem_limit_bytes=63 * 2**20),
    )(*made)
    return (
        jnp.swapaxes(out.reshape(rows, width, channels), 0, 1)[None],
        grad.reshape(pair.shape),
        ggain,
        gproj,
        jnp.swapaxes(gbias, 1, 2),
        gout,
    )


def solution(mesh):
    placed = (
        P(("groups", "dp"), "axial", None, None),
        P(("groups", "dp"), "axial", None),
        P(),
        P(),
        P(),
        P(),
        P(("groups", "dp"), None, "axial", None),
    )
    return jax.shard_map(
        functools.partial(local, mesh.shape["axial"]),
        mesh=mesh,
        in_specs=placed,
        out_specs=(
            P(("groups", "dp"), None, "axial", None),
            P(("groups", "dp"), "axial", None, None),
            P("groups", None),
            P("groups", None, None),
            P("groups", None, None),
            P("groups", None, None),
        ),
        check_vma=False,
    )
```

```python
import functools
import math

import jax
import jax.numpy as jnp
from jax import lax
from jax.experimental import pallas as pl
from jax.experimental.pallas import tpu as pltpu
from jax.sharding import PartitionSpec as P

MESH = pl.DeviceIdType.MESH
F32, BF16 = jnp.float32, jnp.bfloat16
H = 4
EPS = 1e-05
MASKED = -1000000000.0
HIGHEST = lax.Precision.HIGHEST


def dot(a, b, ca, cb, precision=None):
    return lax.dot_general(a, b, (((ca,), (cb,)), ((), ())), precision=precision, preferred_element_type=F32)


def kernel(
    n, rows, width, small, block, chunk,
    pair_in, mask_in, gain_in, wproj_in, wbias_in, wout_in, cot_in,
    out_hbm, grad_hbm, gproj_hbm, gout_hbm, gbias_ref, ggain_ref,
    pair_ref, mask_ref, gain_ref, wproj_ref, wbias_raw, wbias_ref, wout_ref, cot_ref, out_ref, grad_ref, tail_ref,
    xhat, rstd, normed, proj, gate, att, dgated, gated, dproj, x2, dy1, bias, dacc, kept,
    bgat, dsend, drecv, asend, arecv, part, fromcore, half, red, full, tails,
    send_sem, recv_sem, core_send, core_recv, in_sem, out_sem,
):
    me = lax.axis_index("axial")
    core = lax.axis_index("dp")
    other = 1 - core
    channels = pair_ref.shape[1]
    head = channels // H
    scale = 1.0 / math.sqrt(head)
    stack = H if small else 1
    half_rows = n * chunk
    tight = width <= 64 and rows <= 8

    def slot_of(l):
        return l if small else 0

    def steps(low, high, body):
        if small:
            for idx in range(low, high):
                body(idx)
        else:
            lax.fori_loop(low, high, lambda idx, c: (body(idx), c)[1], 0)

    loads = [
        pltpu.make_async_copy(source, target, in_sem.at[idx])
        for idx, (source, target) in enumerate((
            (pair_in, pair_ref), (gain_in, gain_ref), (wbias_in, wbias_raw), (wproj_in, wproj_ref),
            (mask_in, mask_ref), (wout_in, wout_ref), (cot_in, cot_ref),
        ))
    ]
    for load in loads:
        load.start()

    barrier = pltpu.get_barrier_semaphore()

    def greet(off):
        pl.semaphore_signal(barrier, inc=1, device_id={"axial": lax.rem(me + off, n)}, device_id_type=MESH)

    steps(1, n, greet)
    pl.semaphore_signal(barrier, inc=1, device_id={"dp": other}, device_id_type=MESH)

    def axial_copy(phase, off, source, target, slot):
        peer = lax.rem(me + off, n)
        return pltpu.make_async_remote_copy(
            src_ref=source(peer), dst_ref=target(slot),
            send_sem=send_sem.at[phase, off], recv_sem=recv_sem.at[phase, off],
            device_id={"axial": peer}, device_id_type=MESH,
        )

    def start(phase, source, target):
        steps(1, n, lambda off: axial_copy(phase, off, source, target, me).start())

    def finish(phase, source, target):
        steps(1, n, lambda off: axial_copy(phase, off, source, target, lax.rem(me + n - off, n)).wait())

    def core_copy(phase, source, target):
        return pltpu.make_async_remote_copy(
            src_ref=source, dst_ref=target, send_sem=core_send.at[phase], recv_sem=core_recv.at[phase],
            device_id={"dp": other}, device_id_type=MESH,
        )

    def at_row(a):
        return pl.ds(a * width if small else pl.multiple_of(a * width, 16), width)

    def place(token, step):
        peer = ((token.astype(F32) + 0.5) * (1.0 / rows)).astype(jnp.int32)
        return peer * block + (token - peer * rows) * step

    spread = place(lax.broadcasted_iota(jnp.int32, (1, width), 1), rows)
    gather = place(lax.broadcasted_iota(jnp.int32, (width, 1), 0), 1)

    lanes = lax.broadcasted_iota(jnp.int32, (1, channels), 1)
    head_masks = [jnp.where((lanes >= h * head) & (lanes < (h + 1) * head), 1.0, 0.0) for h in range(H)]

    def packing(axis):
        shape = (width, n * 8) if axis == 0 else (n * 8, width)
        token = lax.broadcasted_iota(jnp.int32, (width, 1) if axis == 0 else (1, width), axis)
        peer = ((token.astype(F32) + 0.5) * (1.0 / rows)).astype(jnp.int32)
        spots = lax.broadcasted_iota(jnp.int32, shape, 1 - axis)
        return jnp.where(spots == token + peer * (8 - rows), 1.0, 0.0)

    def stacked(value, first):
        value = value.astype(F32)
        return jnp.concatenate([value * head_masks[first + h] for h in range(stack)], axis=0).astype(BF16)

    def merged(value, first):
        total = value[:width] * head_masks[first]
        for h in range(1, stack):
            total = total + value[h * width : (h + 1) * width] * head_masks[first + h]
        return total

    def prepare(l, x_ref):
        x = x_ref[...].astype(F32)
        centered = x - jnp.mean(x, axis=-1, keepdims=True)
        spread = lax.rsqrt(jnp.mean(centered * centered, axis=-1, keepdims=True) + EPS)
        hat = centered * spread
        xhat[l] = hat
        rstd[l] = jnp.broadcast_to(spread, hat.shape)
        normed[l] = (hat * gain_ref[l : l + 1]).astype(BF16)

        def own_bias(a):
            values = dot(wbias_ref[l], normed[l, at_row(a)], 1, 1)
            if tight:
                for h in range(H):
                    low = (h % 2) * 64
                    bgat[l, me, h // 2, a : a + 1, low : low + width] = values[h : h + 1]
            else:
                bgat[slot_of(l), me * rows + a] = values

        steps(0, rows, own_bias)

    def project(l):
        values = dot(normed[l], wproj_ref[l], 1, 0).astype(BF16)
        proj[l] = values
        gate[l] = jax.nn.sigmoid(values[:, 3 * channels :].astype(F32))

    def bias_source(l):
        return lambda peer: bgat.at[l, me] if tight else bgat.at[slot_of(l), pl.ds(me * rows, rows)]

    def bias_target(l):
        return lambda slot: bgat.at[l, slot] if tight else bgat.at[slot_of(l), pl.ds(slot * rows, rows)]

    def stack_bias(l):
        if tight:
            chosen = packing(0)
            for pair in range(H // 2):
                values = dot(chosen, bgat[l, :, pair].reshape(n * 8, 128), 1, 0, HIGHEST)
                for u in range(2):
                    first = (2 * pair + u) * width
                    bias[l, first : first + width] = values[:, u * 64 : u * 64 + width]
            return
        for h in range(H):
            bias[l, h * width : (h + 1) * width] = bgat[slot_of(l), :, h, :]

    def probabilities(l, a, first, queries, keys):
        scores = dot(queries, keys, 1, 1) * scale + bias[l, first * width : (first + stack) * width]
        scores = jnp.where(mask_ref[a] > 0, scores, MASKED)
        top = jnp.max(scores, axis=-1, keepdims=True)
        weights = jnp.exp(scores - top)
        return weights * (1.0 / jnp.sum(weights, axis=-1, keepdims=True))

    def column(l, a, part_index):
        return proj[l, at_row(a), part_index * channels : (part_index + 1) * channels]

    def forward_row(a):
        keys, values, query = column(0, a, 1), column(0, a, 2), column(0, a, 0)
        total = None
        for first in range(0, H, stack):
            probs = probabilities(0, a, first, stacked(query, first), keys)
            if small:
                kept[a] = probs
            term = merged(dot(probs.astype(BF16), values, 1, 0), first)
            total = term if total is None else total + term
        att[0, at_row(a)] = total

    def backward_row(l, a):
        keys, values, query = column(l, a, 1), column(l, a, 2), column(l, a, 0)
        gates = gate[l, at_row(a)]
        d_row = dgated[at_row(a)]
        d_att = (d_row * gates).astype(BF16)
        keep = mask_ref[a] > 0
        total = d_query = d_keys = d_values = None
        for first in range(0, H, stack):
            queries = stacked(query, first)
            probs = kept[a] if small and l == 0 else probabilities(l, a, first, queries, keys)
            probs_b = probs.astype(BF16)
            d_stack = stacked(d_att, first)
            if l == 1:
                term = merged(dot(probs_b, values, 1, 0), first)
                total = term if total is None else total + term
            d_probs = dot(d_stack, values, 1, 1)
            inner = jnp.sum(probs * d_probs, axis=-1, keepdims=True)
            d_scores = jnp.where(keep, probs * (d_probs - inner), 0.0)
            where = slice(first * width, (first + stack) * width)
            if small and a == 0:
                dacc[where] = d_scores
            else:
                dacc[where] += d_scores
            d_b = d_scores.astype(BF16)
            terms = (merged(dot(d_b, keys, 1, 0), first), dot(d_b, queries, 0, 0), dot(probs_b, d_stack, 0, 0))
            if d_query is None:
                d_query, d_keys, d_values = terms
            else:
                d_query, d_keys, d_values = d_query + terms[0], d_keys + terms[1], d_values + terms[2]
        if l == 1:
            att[1, at_row(a)] = total
        else:
            total = att[0, at_row(a)]
        d_gate = d_row * total * gates * (1.0 - gates)
        dproj[at_row(a), :channels] = (d_query * scale).astype(BF16)
        dproj[at_row(a), channels : 2 * channels] = (d_keys * scale).astype(BF16)
        dproj[at_row(a), 2 * channels : 3 * channels] = d_values.astype(BF16)
        dproj[at_row(a), 3 * channels :] = d_gate.astype(BF16)

    def gate_output(l, x_ref):
        values = (gate[l] * att[l]).astype(BF16)
        gated[l] = values
        return (x_ref[...].astype(F32) + dot(values, wout_ref[l], 1, 0)).astype(BF16)

    def turn_send(index, value_at):
        def turned(base, length):
            total = None
            for a in range(rows):
                spots = lax.broadcasted_iota(jnp.int32, (length, width), 0) + (base - a)
                chosen = jnp.where(spots == spread, 1.0, 0.0).astype(BF16)
                term = dot(chosen, value_at(a), 1, 0)
                total = term if total is None else total + term
            return total.astype(BF16)

        def one(peer):
            asend[slot_of(index), peer] = turned(peer * block, block)

        if small:
            asend[index] = turned(0, n * block).reshape(n, block, channels)
        else:
            steps(0, n, one)
        arecv[slot_of(index), me] = asend[slot_of(index), me]
        start(4 + index, lambda peer: asend.at[slot_of(index), peer], lambda slot: arecv.at[slot_of(index), slot])

    def turn_receive(index, target):
        finish(4 + index, lambda peer: asend.at[slot_of(index), peer], lambda slot: arecv.at[slot_of(index), slot])
        arrived = arecv[slot_of(index)].reshape(n * block, channels)

        def one(a):
            spots = lax.broadcasted_iota(jnp.int32, (width, n * block), 1) - a * rows
            chosen = jnp.where(spots == gather, 1.0, 0.0).astype(BF16)
            target[at_row(a)] = dot(chosen, arrived, 1, 0).astype(BF16)

        steps(0, rows, one)

    def ds_source(l):
        return lambda peer: dsend.at[l, peer] if tight else dsend.at[slot_of(l), pl.ds(peer * rows, rows)]

    def ds_target(l):
        return lambda slot: drecv.at[slot_of(l), slot]

    def send_bias_grad(l):
        if tight:
            chosen = packing(1)
            gap = jnp.zeros((width, 64 - width), F32)
            for pair in range(H // 2):
                first = 2 * pair * width
                both = [dacc[first : first + width], gap, dacc[first + width : first + 2 * width], gap]
                values = dot(chosen, jnp.concatenate(both, axis=1), 1, 0, HIGHEST)
                dsend[l, :, pair] = values.reshape(n, 8, 128)
            drecv[l, me] = dsend[l, me]
        else:
            for h in range(H):
                dsend[slot_of(l), :, h, :] = dacc[h * width : (h + 1) * width]
            drecv[slot_of(l), me] = dsend[slot_of(l), pl.ds(me * rows, rows)]
        start(2 + l, ds_source(l), ds_target(l))

    def weight_grads(l, dy):
        values = dot(normed[l], dproj[...], 0, 0)
        for e in range(4):
            part[l, e * channels : (e + 1) * channels] = values[:, e * channels : (e + 1) * channels]
        part[l, 4 * channels : 5 * channels] = dot(gated[l], dy, 0, 0)

    def core_first(l):
        return core_copy(l, part.at[l, pl.ds(other * half_rows, half_rows)], fromcore.at[l])

    def reduce_source(l):
        return lambda peer: half.at[l, peer]

    def reduce_target(l):
        return lambda slot: red.at[l, slot]

    def core_sum(l):
        core_first(l).wait()
        value = part[l, pl.ds(pl.multiple_of(core * half_rows, 8), half_rows)] + fromcore[l]
        half[l] = value.reshape(n, chunk, channels)
        red[l, me] = half[l, me]
        start(6 + l, reduce_source(l), reduce_target(l))

    def full_source(l):
        return lambda peer: full.at[l, chunk_at(me)]

    def full_target(l):
        return lambda slot: full.at[l, chunk_at(slot)]

    def chunk_at(slot):
        return pl.ds(pl.multiple_of((core * n + slot) * chunk, 8), chunk)

    def half_at(which):
        return pl.ds(pl.multiple_of(which * half_rows, 8), half_rows)

    def axial_sum(l):
        finish(6 + l, reduce_source(l), reduce_target(l))
        full[l, chunk_at(me)] = jnp.sum(red[l], axis=0)
        start(8 + l, full_source(l), full_target(l))

    def core_last(l):
        return core_copy(2 + l, full.at[l, half_at(core)], full.at[l, half_at(core)])

    def core_last_wait(l):
        return core_copy(2 + l, full.at[l, half_at(core)], full.at[l, half_at(other)])

    def layer_norm_grad(l, dn, dy):
        finish(2 + l, ds_source(l), ds_target(l))
        own = jnp.sum(drecv[slot_of(l)], axis=0)
        if tight:
            spare = jnp.zeros((8 - H, width), F32)
            own = [
                jnp.concatenate(
                    [own[h // 2, a : a + 1, (h % 2) * 64 : (h % 2) * 64 + width] for h in range(H)] + [spare], axis=0
                )
                for a in range(rows)
            ]
        extra, bias_grad = [], None
        weights = wbias_ref[l].astype(F32)
        for a in range(rows):
            extra.append(dot(own[a], weights, 0, 0, HIGHEST))
            term = dot(own[a], normed[l, a * width : (a + 1) * width].astype(F32), 1, 0, HIGHEST)
            bias_grad = term if bias_grad is None else bias_grad + term
        dn = dn + jnp.concatenate(extra, axis=0)
        hat = xhat[l]
        gain_grad = jnp.sum(dn * hat, axis=0, keepdims=True)
        d_hat = dn * gain_ref[l : l + 1]
        inner = (
            d_hat
            - jnp.mean(d_hat, axis=-1, keepdims=True)
            - hat * jnp.mean(d_hat * hat, axis=-1, keepdims=True)
        )
        tails[me, l * 8 : l * 8 + H] = bias_grad[:H]
        tails[me, l * 8 + H : l * 8 + 8] = jnp.broadcast_to(gain_grad, (8 - H, channels))
        return (dy.astype(F32) + rstd[l] * inner).astype(BF16)

    stores = []

    def store(idx, source, target):
        stores.append(pltpu.make_async_copy(source, target, out_sem.at[idx]))
        stores[-1].start()

    if tight:
        bgat[:, me] = jnp.zeros((2,) + bgat.shape[2:], F32)
    else:
        dsend[...] = jnp.zeros(dsend.shape, F32)
    if half_rows * 2 > 5 * channels:
        part[...] = jnp.zeros(part.shape, F32)

    for load in loads[:3]:
        load.wait()
    for l in range(2):
        spare = jnp.zeros((8 - H, channels), F32)
        wbias_ref[l] = jnp.concatenate([wbias_raw[l].astype(F32), spare], axis=0).astype(BF16)
    prepare(0, pair_ref)
    pl.semaphore_wait(barrier, n)
    start(0, bias_source(0), bias_target(0))
    loads[3].wait()
    project(0)
    finish(0, bias_source(0), bias_target(0))
    stack_bias(0)
    for load in loads[4:]:
        load.wait()
    steps(0, rows, forward_row)
    asend_value = gate_output(0, pair_ref)
    turn_send(0, lambda a: asend_value[a * width : (a + 1) * width])
    dgated[...] = dot(cot_ref[...], wout_ref[1], 1, 1)
    turn_receive(0, x2)

    prepare(1, x2)
    start(1, bias_source(1), bias_target(1))
    project(1)
    finish(1, bias_source(1), bias_target(1))
    stack_bias(1)
    if not small:
        dacc[...] = jnp.zeros(dacc.shape, F32)
    steps(0, rows, functools.partial(backward_row, 1))
    send_bias_grad(1)
    out_ref[...] = gate_output(1, x2)
    store(0, out_ref, out_hbm)
    dn = dot(dproj[...], wproj_ref[1], 1, 1)
    weight_grads(1, cot_ref[...])
    core_first(1).start()
    d_columns = layer_norm_grad(1, dn, cot_ref[...])
    turn_send(1, lambda a: d_columns[a * width : (a + 1) * width])
    core_sum(1)
    turn_receive(1, dy1)

    dgated[...] = dot(dy1[...], wout_ref[0], 1, 1)
    if not small:
        dacc[...] = jnp.zeros(dacc.shape, F32)
    steps(0, rows, functools.partial(backward_row, 0))
    send_bias_grad(0)
    axial_sum(1)
    weight_grads(0, dy1[...])
    core_first(0).start()
    dn = dot(dproj[...], wproj_ref[0], 1, 1)
    core_sum(0)
    axial_sum(0)
    grad_ref[...] = layer_norm_grad(0, dn, dy1[...])
    store(1, grad_ref, grad_hbm)
    start(10, lambda peer: tails.at[me], lambda slot: tails.at[slot])
    finish(8 + 1, full_source(1), full_target(1))
    core_last(1).start()
    finish(10, lambda peer: tails.at[me], lambda slot: tails.at[slot])
    mine = jnp.sum(tails[...], axis=0)
    tail_ref[0] = mine
    core_copy(4, tail_ref.at[0], tail_ref.at[1]).start()
    finish(8, full_source(0), full_target(0))
    core_last(0).start()
    core_copy(4, tail_ref.at[0], tail_ref.at[1]).wait()
    tail_ref[0] = tail_ref[0] + tail_ref[1]
    for l in range(2):
        gbias_ref[l] = tail_ref[0, l * 8 : l * 8 + H]
        ggain_ref[l : l + 1] = tail_ref[0, l * 8 + H : l * 8 + H + 1]
    for l in (1, 0):
        core_last_wait(l).wait()
        for e in range(4):
            store(
                2 + 5 * l + e, full.at[l, pl.ds(e * channels, channels)],
                gproj_hbm.at[l, :, pl.ds(e * channels, channels)],
            )
        store(6 + 5 * l, full.at[l, pl.ds(4 * channels, channels)], gout_hbm.at[l])
    for copy in stores:
        copy.wait()


def hand_over(*refs):
    sources, targets, held, semaphore = refs[:6], refs[6:12], refs[12:18], refs[18]
    inward = [pltpu.make_async_copy(sources[idx], held[idx], semaphore.at[0, idx]) for idx in range(6)]
    outward = [pltpu.make_async_copy(held[idx], targets[idx], semaphore.at[1, idx]) for idx in range(6)]
    for copy in inward:
        copy.start()
    for idx in range(6):
        inward[idx].wait()
        outward[idx].start()
    for copy in outward:
        copy.wait()


def local(n, pair, pair_mask, ln_gain, projection_weight, pair_bias_weight, w_out, cotangent):
    rows, width, channels = pair.shape[1:]
    small = width <= 128
    slots = 2 if small else 1
    tight = width <= 64 and rows <= 8
    block = -(-rows * rows // 16) * 16
    chunk = -(-5 * channels // (2 * n * 8)) * 8
    wbias = jnp.swapaxes(pair_bias_weight, 1, 2)
    cot = jnp.swapaxes(cotangent[0], 0, 1).reshape(rows * width, channels)
    size = rows * width
    shape = jax.ShapeDtypeStruct
    vmem = pltpu.VMEM
    whole = pl.BlockSpec(memory_space=pltpu.VMEM)
    hbm = pl.BlockSpec(memory_space=pltpu.HBM)
    results = (
        shape((size, channels), BF16),
        shape((size, channels), BF16),
        shape((2, channels, 4 * channels), F32),
        shape((2, channels, channels), F32),
        shape((2, H, channels), F32),
        shape((2, channels), F32),
    )
    made = pl.pallas_call(
        functools.partial(kernel, n, rows, width, small, block, chunk),
        out_shape=results,
        in_specs=[hbm] * 7,
        out_specs=(hbm,) * 4 + (whole,) * 2,
        scratch_shapes=[
            vmem((size, channels), BF16),
            vmem((rows, 1, width), jnp.int32),
            vmem((2, channels), F32),
            vmem((2, channels, 4 * channels), BF16),
            vmem((2, H, channels), BF16),
            vmem((2, 8, channels), BF16),
            vmem((2, channels, channels), BF16),
            vmem((size, channels), BF16),
            vmem((size, channels), BF16),
            vmem((size, channels), BF16),
            vmem((2, 16, channels), F32),
            vmem((2, size, channels), F32),
            vmem((2, size, channels), F32),
            vmem((2, size, channels), BF16),
            vmem((2, size, 4 * channels), BF16),
            vmem((2, size, channels), F32),
            vmem((2, size, channels), F32),
            vmem((size, channels), F32),
            vmem((2, size, channels), BF16),
            vmem((size, 4 * channels), BF16),
            vmem((size, channels), BF16),
            vmem((size, channels), BF16),
            vmem((2, H * width, width), F32),
            vmem((H * width, width), F32),
            vmem((rows, H * width, width) if small else (1, 8, 128), F32),
            vmem((2, n, 2, 8, 128) if tight else (slots, width, 8, width), F32),
            vmem((2, n, 2, 8, 128) if tight else (slots, width, 8, width), F32),
            vmem((2, n, 2, 8, 128) if tight else (slots, n, rows, 8, width), F32),
            vmem((slots, n, block, channels), BF16),
            vmem((slots, n, block, channels), BF16),
            vmem((2, 2 * n * chunk, channels), F32),
            vmem((2, n * chunk, channels), F32),
            vmem((2, n, chunk, channels), F32),
            vmem((2, n, chunk, channels), F32),
            vmem((2, 2 * n * chunk, channels), F32),
            vmem((n, 16, channels), F32),
            pltpu.SemaphoreType.DMA((11, n)),
            pltpu.SemaphoreType.DMA((11, n)),
            pltpu.SemaphoreType.DMA((5,)),
            pltpu.SemaphoreType.DMA((5,)),
            pltpu.SemaphoreType.DMA((7,)),
            pltpu.SemaphoreType.DMA((12,)),
        ],
        compiler_params=pltpu.CompilerParams(
            collective_id=0, has_side_effects=True, vmem_limit_bytes=63 * 2**20
        ),
    )(pair.reshape(size, channels), pair_mask.reshape(rows, 1, width), ln_gain, projection_weight, wbias, w_out, cot)
    out, grad, gproj, gout, gbias, ggain = pl.pallas_call(
        hand_over,
        out_shape=results,
        in_specs=[hbm] * 6,
        out_specs=(hbm,) * 6,
        scratch_shapes=[vmem(item.shape, item.dtype) for item in results] + [pltpu.SemaphoreType.DMA((2, 6))],
        compiler_params=pltpu.CompilerParams(vmem_limit_bytes=63 * 2**20),
    )(*made)
    return (
        jnp.swapaxes(out.reshape(rows, width, channels), 0, 1)[None],
        grad.reshape(pair.shape),
        ggain,
        gproj,
        jnp.swapaxes(gbias, 1, 2),
        gout,
    )


def solution(mesh):
    placed = (
        P(("groups", "dp"), "axial", None, None),
        P(("groups", "dp"), "axial", None),
        P(),
        P(),
        P(),
        P(),
        P(("groups", "dp"), None, "axial", None),
    )
    return jax.shard_map(
        functools.partial(local, mesh.shape["axial"]),
        mesh=mesh,
        in_specs=placed,
        out_specs=(
            P(("groups", "dp"), None, "axial", None),
            P(("groups", "dp"), "axial", None, None),
            P("groups", None),
            P("groups", None, None),
            P("groups", None, None),
            P("groups", None, None),
        ),
        check_vma=False,
    )
```
